128 devices in a mesh: row: 8 (over y, z_hi), col: 16 (over x, z_lo, core).
Axes of the slice: x: 4, y: 4, z: 4 (z_hi: 2, z_lo: 2; z = z_hi * 2 + z_lo), core: 2. Of those that a mesh axis runs over, the one named last changes fastest.
Arguments:
- front_matrix: float32 [16384, 16384], P('row', 'col'), may hold values from -6 to 206
- updates: float32 [16384, 16384], P('row', 'col'), may hold values from -6 to 6
- child_map: int32 [4, 64], replicated, may hold values from 0 to 127, as said below
Outputs:
- factored: float32 [16384, 16384], P('row', 'col')
The draws below stay inside these ranges and needn't reach their ends.
Inputs may be any that keep to these rules, and one draw needn't show every extreme that they name: `child_map`: entries of each row are distinct. For every child and every g below 8, the entries g * 8 to (g+1) * 8 - 1 are increasing, leave the remainder g modulo 8, and their quotients by 16 are distinct. Counting the blocks of one device's share of updates by the device that owns their parent block in the contiguous 8 x 16 layout of the front, no device sends more than 2 blocks to one device, and some device sends exactly 2 in every draw.
All inputs are finite; a program needn't handle non-finite values.
Results may differ from the reference program's by a relative error of at most 0.00005.
Values sent between devices are 32-bit elements; how exact they have to be, the bound alone decides.
No kernel may reach another device: no remote copies, remote signals or barrier semaphores. Data moves between devices by JAX's collectives and lax.ppermute only.
A program may use at most 192 MiB of HBM per device.

```python
import jax
import jax.numpy as jnp
from jax import lax

BS = 128
NCHILD = 4
PROWS = 8
PCOLS = 16
FB = 128
ORDER = 16384
CB = 64


def pick_groups(key):
    pair_count = PCOLS // 2
    bits = jax.random.randint(key, (PROWS, pair_count), 0, 2)
    chosen = 2 * jnp.arange(pair_count)[None, :] + bits
    return (PROWS * chosen + jnp.arange(PROWS)[:, None]).reshape(-1).astype(jnp.int32)


def draw_child_map(key, part):
    key = jax.random.fold_in(key, 23)
    return jax.vmap(pick_groups)(jax.random.split(key, NCHILD))


def draw_front_matrix(key, part):
    key = jax.random.fold_in(key, 11)
    order_total = FB * BS
    noise_key, diag_key = jax.random.split(key)
    jitter = jax.random.truncated_normal(noise_key, -6.0, 6.0, (order_total, order_total), jnp.float32)
    diag_boost = jax.random.uniform(diag_key, (order_total,), jnp.float32, 100.0, 200.0)
    on_diagonal = jnp.arange(order_total)[:, None] == jnp.arange(order_total)[None, :]
    return jitter + jnp.where(on_diagonal, diag_boost[None, :], 0.0)


def level_of(rng, dims, pieces, smallest, largest):
    def one(axis_at, blocks):
        steps = jax.random.uniform(jax.random.fold_in(jax.random.fold_in(rng, 6), axis_at), (blocks,), jnp.float32, smallest / len(pieces), largest / len(pieces))
        return jnp.repeat(jnp.exp(steps), dims[axis_at] // blocks).reshape((-1,) + (1,) * (len(dims) - axis_at - 1))

    gain = one(*pieces[0])
    for cut in pieces[1:]:
        gain = gain * one(*cut)
    return gain


def bell_draw(stream_key, extent, deviation, reach, cuts=(), dtype=jnp.bfloat16):
    drawn = jax.random.normal(stream_key, extent, jnp.float32) * deviation
    if len(cuts) > 0:
        drawn = level_of(stream_key, extent, cuts, -0.22, 0.18) * drawn
    return jnp.clip(drawn, min=-reach, max=reach).astype(dtype)


def setup_inputs(seed: int = 0) -> dict:
    streams_of = jax.random.split(jax.random.key(seed), 4)
    front_matrix = draw_front_matrix(jax.random.fold_in(streams_of[3], 71), 0)
    updates = bell_draw(streams_of[1], (ORDER, ORDER), 1.0, 6.0, ((0, 8), (1, 16)), jnp.float32)
    child_map = draw_child_map(jax.random.fold_in(streams_of[3], 71), 0)
    return {"front_matrix": front_matrix, "updates": updates, "child_map": child_map}


def reference(front_matrix, updates, child_map):
    child_order = CB * BS
    blocks = front_matrix.reshape(FB, BS, FB, BS)
    for child_id in range(NCHILD):
        row_half = child_id % 2
        col_half = child_id // 2
        child_part = updates[row_half * child_order:(row_half + 1) * child_order, col_half * child_order:(col_half + 1) * child_order]
        child_part = child_part.reshape(CB, BS, CB, BS).transpose(0, 2, 1, 3)
        mapped = child_map[child_id].astype(jnp.int32)
        blocks = blocks.at[mapped[:, None], :, mapped[None, :], :].add(child_part)
    extended = blocks.reshape(FB * BS, FB * BS)
    factor_head = jnp.linalg.cholesky(extended[:BS, :BS])
    panel = lax.linalg.triangular_solve(factor_head, extended[:, :BS], left_side=False, lower=True, transpose_a=True)
    panel = panel.at[:BS].set(factor_head)
    trailing = extended[BS:, BS:] - jnp.dot(panel[BS:].astype(jnp.float32), panel[BS:].T.astype(jnp.float32), precision=lax.Precision.HIGHEST, preferred_element_type=jnp.float32)
    factored = extended.at[BS:, BS:].set(trailing)
    factored = factored.at[:, :BS].set(panel)
    return factored
```

```python
import functools

import jax
import jax.numpy as jnp
from jax import lax
from jax.experimental import pallas as pl
from jax.experimental.pallas import tpu as pltpu
from jax.sharding import Mesh
from jax.sharding import PartitionSpec as P

CHIP = ("y", "zh", "x", "zl")
ALL = CHIP + ("core",)
CHUNKS = 2


def dev(row, col, core):
    return (row * 8 + col) * 2 + core


def child_sums(flags, blocks, own_out, sib_out):
    sr, g = pl.program_id(0), pl.program_id(1)
    groups = pl.num_programs(1)
    for scp in range(4):
        for half in range(2):
            own = jnp.zeros(own_out.shape[-2:], jnp.float32)
            sib = jnp.zeros(own_out.shape[-2:], jnp.float32)
            for h in range(2):
                for v in range(2):
                    child = h + 2 * v
                    at = ((((child * 4 + sr) * groups + g) * 4 + scp) * 2 + half) * 2
                    block = blocks[h, 0, v, scp, 0]
                    own += flags[at] * block
                    sib += flags[at + 1] * block
            own_out[half, 0, 0, scp] = own
            sib_out[half, 0, 0, scp] = sib


def add_sums(core, base, own, sib, out):
    bs = own.shape[-1]
    first = core[0] == 0
    for scp in range(4):
        mine, other = own[0, 0, 0, scp], sib[0, 0, 0, scp]
        left, right = pl.ds(2 * scp * bs, bs), pl.ds((2 * scp + 1) * bs, bs)
        out[0, :, left] = base[0, :, left] + jnp.where(first, mine, other)
        out[0, :, right] = base[0, :, right] + jnp.where(first, other, mine)


def run_child_sums(flags, recv, groups, rows, bs):
    recv = recv.reshape(2, 4, 2, 4, groups, rows, bs)
    part = jax.ShapeDtypeStruct((2, 4, groups, 4, rows, bs), jnp.float32)
    spec = pl.BlockSpec((2, 1, 1, 4, rows, bs), lambda sr, g, *_: (0, sr, g, 0, 0, 0))
    return pl.pallas_call(
        child_sums,
        out_shape=(part, part),
        grid_spec=pltpu.PrefetchScalarGridSpec(
            num_scalar_prefetch=1,
            grid=(4, groups),
            in_specs=[pl.BlockSpec((2, 1, 2, 4, 1, rows, bs), lambda sr, g, *_: (0, sr, 0, 0, g, 0, 0))],
            out_specs=(spec, spec),
        ),
        compiler_params=pltpu.CompilerParams(vmem_limit_bytes=32 << 20),
        cost_estimate=pl.CostEstimate(flops=8 * recv.size, bytes_accessed=8 * recv.size, transcendentals=0),
        name="child_sums",
    )(flags, recv)


def run_add_sums(core, base, own, sib, first_group, groups, row_at, rows, bs):
    cols = base.shape[-1]
    place = pl.BlockSpec((1, rows, cols), lambda half, sr, g, *_: (8 * half + 2 * sr + first_group + g, row_at, 0))
    part = pl.BlockSpec((1, 1, 1, 4, rows, bs), lambda half, sr, g, *_: (half, sr, g, 0, 0, 0))
    return pl.pallas_call(
        add_sums,
        out_shape=jax.ShapeDtypeStruct(base.shape, jnp.float32),
        grid_spec=pltpu.PrefetchScalarGridSpec(
            num_scalar_prefetch=1,
            grid=(2, 4, groups),
            in_specs=[place, part, part],
            out_specs=place,
        ),
        input_output_aliases={1: 0},
        compiler_params=pltpu.CompilerParams(vmem_limit_bytes=32 << 20),
        cost_estimate=pl.CostEstimate(flops=2 * own.size, bytes_accessed=24 * own.size, transcendentals=0),
        name="add_sums",
    )(core, base, own, sib)


def body(front, updates, child_map):
    rows_dev, cols_dev = front.shape
    bs = rows_dev // 16
    y, zh, x, zl, t = (lax.axis_index(a) for a in ALL)
    ji, jc = 2 * y + zh, 2 * x + zl
    col = 2 * jc + t
    bits = (child_map.reshape(4, 8, 8) // 8) % 2
    take = functools.partial(lax.dynamic_index_in_dim, keepdims=False)

    child = y // 2 + 2 * (x // 2)
    sr_me = 2 * (y % 2) + zh
    is_corner = (ji == 0) & (col == 0)
    head_bit = take(bits[:, 0, 0], child, 0)
    live = (head_bit == 0).astype(jnp.float32)
    ucol = updates[:, :bs].reshape(2, 8, bs, bs) * live
    fcol = front[:, :bs]
    corner = ucol[0, 0] + jnp.where(is_corner, fcol[:bs], 0.0)
    sources = [(r, v) for r in range(8) for v in range(2)]
    landed = []
    for k in range(8):
        to = (k + 2 * child) % 8
        load = jnp.concatenate([take(ucol, to, 1), corner[None]])
        pairs = []
        for r, v in sources:
            c = r // 4 + 2 * v
            pairs.append((dev(r, 4 * v, 0), dev((k + 2 * c) % 8, 2 * (r % 4), 0)))
        landed.append(lax.ppermute(load, ALL, pairs))
    fq = fcol.reshape(2, 4, 2, bs, bs)
    front_part = jnp.where(x == 0, fq[:, 0], 0.0)
    for q in range(1, 4):
        pairs = [(dev(r, 0, 0), dev(r, 2 * q, 0)) for r in range(8)]
        front_part = front_part + lax.ppermute(fq[:, q], ALL, pairs)
    landed = jnp.stack(landed)
    e00 = jnp.zeros((bs, bs), jnp.float32)
    owned = front_part
    row_bits = lax.dynamic_slice_in_dim(take(bits, ji, 2), 2 * x, 2, 1)
    for c in range(4):
        piece = take(landed, (ji - 2 * c) % 8, 0)
        mask = (row_bits[c][None, :] == jnp.arange(2)[:, None]).astype(jnp.float32)
        owned = owned + mask[:, :, None, None] * piece[None, :2]
        e00 = e00 + piece[2]
    load = jnp.concatenate([owned.reshape(4, bs, bs), e00[None]])
    got = lax.ppermute(load, ALL, [(dev(r, 2 * q, 0), dev(r, 2 * q, 1)) for r in range(8) for q in range(4)])
    load = jnp.where(t == 0, load, got)
    mine = jnp.where(t == 0, load[0:2], load[2:4])
    load = jnp.concatenate([mine, load[4:]])
    along = []
    for dx in range(4):
        total = jnp.where(zl == 0, load, 0.0) if dx == 0 else None
        for dz in range(2):
            if dx == 0 and dz == 0:
                continue
            pairs = [
                (dev(r, 2 * q, core), dev(r, 2 * ((q + dx) % 4) + dz, core))
                for r in range(8) for q in range(4) for core in range(2)
            ]
            got = lax.ppermute(load, ALL, pairs)
            total = got if total is None else total + got
        along.append(total)
    along = jnp.stack(along)
    pieces = [take(along, (x - q) % 4, 0) for q in range(4)]
    head_raw = pieces[0][2]
    half_slab = jnp.concatenate([p[:2] for p in pieces])
    other_half = lax.ppermute(half_slab, "core", [(0, 1), (1, 0)])
    slab = jnp.where(t == 0, jnp.stack([half_slab, other_half]), jnp.stack([other_half, half_slab]))
    slab = slab.reshape(rows_dev, bs)
    down = []
    for k in range(8):
        pairs = [
            (dev(r, 2 * q, core), dev((k + 2 * q) % 8, r, core))
            for r in range(8) for q in range(4) for core in range(2)
        ]
        down.append(lax.ppermute(mine, ALL, pairs))
    down = jnp.stack(down)
    col_slab = jnp.concatenate([take(down, (ji - 2 * q) % 8, 0) for q in range(4)]).reshape(cols_dev, bs)

    head = jnp.linalg.cholesky(head_raw)
    solved = lax.linalg.triangular_solve(
        head, jnp.concatenate([slab, col_slab]), left_side=False, lower=True, transpose_a=True
    )
    panel, col_panel = solved[:rows_dev], solved[rows_dev:]
    product = jnp.dot(panel, col_panel.T, precision=lax.Precision.HIGHEST, preferred_element_type=jnp.float32)
    in_rows = (ji * rows_dev + jnp.arange(rows_dev)) >= bs
    in_cols = (col * cols_dev + jnp.arange(cols_dev)) >= bs
    base = jnp.where(in_rows[:, None] & in_cols[None, :], front - product, front)
    panel = panel.at[:bs].set(jnp.where(ji == 0, head, panel[:bs]))
    base = base.at[:, :bs].set(jnp.where(col == 0, panel, base[:, :bs]))
    base = base.reshape(16, bs, cols_dev)

    groups = 2 if CHUNKS == 1 else 1
    parts = max(CHUNKS // 2, 1)
    rows = bs // parts
    core_id = t.reshape(1).astype(jnp.int32)
    col_bits = take(take(bits, jc, 2).reshape(4, 4, 2), t, 2)
    row_bits = take(bits, ji, 2).reshape(4, 4, 2)
    to_own = col_bits == t
    in_panel = (col == 0) & (jnp.arange(4) == 0)
    send = updates.reshape(2, 8, bs, 8, bs)
    for gi in range(0, 2, groups):
        for part in range(parts):
            block = send[gi:gi + groups, :, part * rows:(part + 1) * rows].transpose(1, 3, 0, 2, 4)
            recv = lax.all_to_all(block.reshape(64, groups * rows, bs), CHIP, 0, 0, tiled=True)
            here = (row_bits[:, :, gi:gi + groups, None, None] == jnp.arange(2))
            own = (to_own & ~in_panel)[:, None, None, :, None] & here
            sib = (~to_own)[:, None, None, :, None] & here
            flags = jnp.stack([own, sib], -1).astype(jnp.float32).reshape(-1)
            own_sum, sib_sum = run_child_sums(flags, recv, groups, rows, bs)
            sib_sum = lax.ppermute(sib_sum, "core", [(0, 1), (1, 0)])
            base = run_add_sums(core_id, base, own_sum, sib_sum, gi, groups, part, rows, bs)
    return base.reshape(rows_dev, cols_dev)


def solution(mesh):
    fine = Mesh(mesh.devices.reshape(4, 2, 4, 2, 2), ALL)
    spec = P(("y", "zh"), ("x", "zl", "core"))
    return jax.shard_map(body, mesh=fine, in_specs=(spec, spec, P()), out_specs=spec, check_vma=False)
```

```python
import jax
import jax.numpy as jnp
from jax import lax
from jax.experimental import pallas as pl
from jax.experimental.pallas import tpu as pltpu
from jax.sharding import Mesh
from jax.sharding import PartitionSpec as P

CHIP = ("y", "zh", "x", "zl")
ALL = CHIP + ("core",)
CORE_SWAP = [(0, 1), (1, 0)]
VMEM = pl.BlockSpec(memory_space=pltpu.VMEM)
SMEM = pl.BlockSpec(memory_space=pltpu.SMEM)
HBM = pl.BlockSpec(memory_space=pltpu.HBM)
F32 = jnp.float32


def call(kernel, out_shape, in_specs, out_specs, name, moved, scratch=(), aliases=None, limit=16):
    many = isinstance(out_shape, tuple)
    outs = zip(out_shape, out_specs) if many else ((out_shape, out_specs),)
    outs = tuple(pltpu.HBM(array.shape, array.dtype) if spec is HBM else array for array, spec in outs)
    run = pl.pallas_call(
        kernel,
        out_shape=outs if many else outs[0],
        in_specs=in_specs,
        out_specs=out_specs,
        scratch_shapes=scratch,
        input_output_aliases=aliases or {},
        compiler_params=pltpu.CompilerParams(vmem_limit_bytes=limit << 20),
        cost_estimate=pl.CostEstimate(flops=0, bytes_accessed=moved, transcendentals=0),
        name=name,
    )

    def placed(*args):
        return run(*(
            pltpu.with_memory_space_constraint(arg, pltpu.HBM) if spec is HBM else arg
            for arg, spec in zip(args, in_specs)
        ))

    return placed


def shape(*dims):
    return jax.ShapeDtypeStruct(dims, F32)


TOKEN = shape(8, 128)


def run_lift(updates, front, bs):
    rows = updates.shape[0]
    half = bs // 2

    def lift(updates, front, low, high, token, ucol, fcol, sems):
        copies = [
            pltpu.make_async_copy(whole.at[:, pl.ds(0, bs)], part, sems.at[i])
            for i, (whole, part) in enumerate(((updates, ucol), (front, fcol)))
        ]
        for copy in copies:
            copy.start()
        token[...] = jnp.zeros_like(token)
        for at, (copy, part) in enumerate(zip(copies, (ucol, fcol))):
            copy.wait()

            def one(chip, carry):
                low[chip, 16 * at:16 * at + 16] = part[pl.ds(chip, 16, stride=bs), :]
                high[chip, 16 * at:16 * at + 16] = part[pl.ds(half + chip, 16, stride=bs), :]
                return carry

            lax.fori_loop(0, half, one, 0, unroll=4)

    share = shape(half, 32, bs)
    return call(
        lift, (share, share, TOKEN), [HBM, HBM], (VMEM,) * 3, "lift", 16 * rows * bs,
        [pltpu.VMEM((rows, bs), F32), pltpu.VMEM((rows, bs), F32), pltpu.SemaphoreType.DMA((2,))],
    )(updates, front)


def run_pack(blocks, wait, gi, at, rows, extra):
    bs = blocks.shape[1]

    def pack(blocks, wait, out, held, read_sems, write_sems):
        def read(j):
            return pltpu.make_async_copy(blocks.at[8 * gi + j, pl.ds(at, rows)], held.at[j], read_sems.at[j])

        def write(j, jc):
            lanes = pl.ds(jc * bs, bs)
            return pltpu.make_async_copy(
                held.at[j, :, lanes], out.at[8 * j + jc, pl.ds(0, rows)], write_sems.at[8 * j + jc]
            )

        for j in range(8):
            read(j).start()
        for j in range(8):
            read(j).wait()
            for jc in range(8):
                write(j, jc).start()
        for j in range(8):
            for jc in range(8):
                write(j, jc).wait()

    return call(
        pack, shape(64, rows + extra, bs), [HBM, VMEM], HBM, "pack", 512 * rows * bs,
        [pltpu.VMEM((8, rows, 8 * bs), F32), pltpu.SemaphoreType.DMA((8,)), pltpu.SemaphoreType.DMA((64,))],
    )(blocks, wait)


def run_put_rows(load, low, other, core, rows):
    def put_rows(core, load, low, other, out, token, sem):
        token[...] = jnp.zeros_like(token)
        for c, part in ((0, low), (1, other)):
            @pl.when(core[0] == c)
            def _():
                copy = pltpu.make_async_copy(part, out.at[:, pl.ds(rows, 32)], sem)
                copy.start()
                copy.wait()

    return call(
        put_rows, (shape(*load.shape), TOKEN), [SMEM, HBM, VMEM, VMEM], (HBM, VMEM), "put_rows", 8 * other.size,
        [pltpu.SemaphoreType.DMA], aliases={1: 0},
    )(core, load, low, other)


def run_sum_rows(marks, recv, load, first, last):
    bs = recv.shape[-1]

    def sum_rows(marks, recv, load, out, token, kids, total, rows, sem):
        token[...] = jnp.zeros_like(token)
        for up in range(2):
            for sr in range(4):
                acc = jnp.zeros((16, bs), F32)
                for h in range(2):
                    for v in range(2):
                        acc += marks[up, sr, 2 * v + h] * recv[(4 * h + sr) * 8 + 4 * v, first:first + 16]
                kids[pl.ds((up * 4 + sr) * 16, 16)] = acc
        for j in range(8):
            total[j] = kids[pl.ds(j, 16, stride=8), :] + recv[8 * j, first + 16:first + 32]
        corner = total[0, 0:8]
        for j in range(8):
            for jc in range(8):
                at = 8 * j + jc
                rows[at, 0:16] = total[j]
                rows[at, 16:32] = total[jc]
                rows[at, 32:40] = corner
        copy = pltpu.make_async_copy(rows, out.at[:, pl.ds(last, 40)], sem)
        copy.start()
        copy.wait()

    return call(
        sum_rows, (shape(*load.shape), TOKEN), [VMEM, VMEM, HBM], (HBM, VMEM), "sum_rows", 64 * 40 * bs * 8,
        [pltpu.VMEM((128, bs), F32), pltpu.VMEM((8, 16, bs), F32), pltpu.VMEM((64, 40, bs), F32), pltpu.SemaphoreType.DMA],
        aliases={2: 0},
    )(marks, recv, load)


def add_blocks(flags, recv, sr, scp, here, sides):
    sums = {}
    for h in range(2):
        for v in range(2):
            block = recv[(4 * h + sr) * 8 + 4 * v + scp, here]
            for up in range(2):
                for side in sides:
                    term = flags[((((h + 2 * v) * 4 + sr) * 4 + scp) * 2 + up) * 2 + side] * block
                    sums[up, side] = sums[up, side] + term if (up, side) in sums else term
    return sums


def child_sums(flags, recv, own, sib):
    rows, step = own.shape[3], 32

    def one(i, carry):
        sr, at = i // (rows // step), pl.multiple_of(i % (rows // step) * step, step)
        for scp in range(4):
            sums = add_blocks(flags, recv, sr, scp, pl.ds(at, step), (0, 1))
            for up in range(2):
                own[up, sr, scp, pl.ds(at, step)] = sums[up, 0]
                sib[up, sr, scp, pl.ds(at, step)] = sums[up, 1]
        return carry

    lax.fori_loop(0, 4 * (rows // step), one, 0)


def run_child_sums(flags, recv, wait, rows, bs):
    def kernel(flags, recv, wait, own, sib, token):
        token[...] = jnp.zeros_like(token)
        child_sums(flags, recv, own, sib)

    part = shape(2, 4, 4, rows, bs)
    return call(
        kernel, (part, part, TOKEN), [SMEM, VMEM, VMEM], (VMEM,) * 3, "child_sums", 64 * rows * bs * 8,
    )(flags, recv, wait)


def run_assemble(core, flags, mine, other, first):
    chips, width, bs = mine.shape
    half = bs // 2

    def assemble(core, flags, flat, mine, other, out, corner, own, sib):
        t = core[0]
        for who, (part, span, at) in enumerate(((flat, width, first), (other, 40, 0))):
            rows_at = pl.multiple_of(half * (t if who == 0 else 1 - t), half)
            for s in range(25):
                start = at + s if s < 16 else at + s + 8 * t if s < 24 else at + 32
                rows = part[pl.ds(start, half, stride=span), :]
                if s < 24:
                    out[s, pl.ds(rows_at, half)] = rows
                else:
                    corner[pl.ds(rows_at, half)] = rows
        child_sums(flags, mine, own, sib)

    part = shape(2, 4, 4, first, bs)
    return call(
        assemble, (shape(24, bs, bs), shape(bs, bs), part, part), [SMEM, SMEM, VMEM, VMEM, VMEM], (VMEM,) * 4, "assemble",
        200 * bs * bs,
    )(core, flags, mine.reshape(chips * width, bs), mine, other.reshape(chips * 40, bs))


def split(a):
    high = a.astype(jnp.bfloat16)
    left = a - high.astype(F32)
    mid = left.astype(jnp.bfloat16)
    return high, mid, (left - mid.astype(F32)).astype(jnp.bfloat16)


def spread(left, mine, other):
    return jnp.where(left, mine, other), jnp.where(left, other, mine)


def pair(scp, bs):
    return slice(2 * scp * bs, (2 * scp + 1) * bs), slice((2 * scp + 1) * bs, (2 * scp + 2) * bs)


def run_base(edge, front, solved, head, early, bs):
    rows, cols = front.shape
    blocks, tile, step = rows // bs, 256, 32
    cut = early[0].shape[3]

    def base(edge, front, solved, head, own0, sib0, own1, sib1, out, rest, token, held, right, sems, back):
        top, col_zero, left = edge[0] == 1, edge[1] == 1, edge[2] == 0
        token[...] = jnp.zeros_like(token)

        def room(i):
            return held.at[i // 2] if i % 2 == 0 else rest.at[i // 2]

        for i in range(blocks):
            pltpu.make_async_copy(front.at[i], room(i), sems.at[i]).start()

        for at in range(0, cols, bs):
            high, mid, low = split(solved[rows + at:rows + at + bs])
            right[at:at + bs] = jnp.concatenate([high, high, mid, high, mid, low], axis=1)

        def less(i, to, sem, n):
            pltpu.make_async_copy(front.at[i], to.at[n], sem).wait()
            own = solved[pl.ds(pl.multiple_of(i * bs, bs), bs)]
            high, mid, low = split(own)
            parts = jnp.concatenate([high, mid, high, low, mid, high], axis=1)
            keep = jnp.where(top & (i == 0), 0.0, 1.0)
            for at in range(0, cols, tile):
                lanes = slice(at, at + tile)
                product = lax.dot_general(
                    parts, right[at:at + tile], (((1,), (1,)), ((), ())), preferred_element_type=F32
                )
                to[n, :, lanes] -= keep * product

            @pl.when(col_zero)
            def _():
                to[n, :, 0:bs] = own

            @pl.when(top & col_zero & (i == 0))
            def _():
                to[n, :, 0:bs] = head[...]

        def write(n):
            return pltpu.make_async_copy(held.at[n], out.at[n, pl.ds(0, bs)], back.at[n])

        def one(n, carry):
            less(2 * n, held, sems.at[2 * n], n)
            up, sr = n // 4, n % 4
            for at in range(0, bs, step):
                here = slice(at, at + step)
                own, sib, inner = (own0, sib0, at) if at < cut else (own1, sib1, at - cut)
                for scp in range(4):
                    two = spread(left, own[up, sr, scp, inner:inner + step], sib[up, sr, scp, inner:inner + step])
                    for lanes, add in zip(pair(scp, bs), two):
                        held[n, here, lanes] += add
            write(n).start()
            less(2 * n + 1, rest, sems.at[2 * n + 1], n)
            return carry

        lax.fori_loop(0, blocks // 2, one, 0)
        lax.fori_loop(0, blocks // 2, lambda n, c: (write(n).wait(), c)[1], 0)

    return call(
        base, (shape(blocks // 2, 2 * bs, cols), shape(blocks // 2, bs, cols), TOKEN), [SMEM, HBM] + [VMEM] * 6,
        (HBM, VMEM, VMEM), "base", rows * cols * 8,
        [pltpu.VMEM((blocks // 2, bs, cols), F32), pltpu.VMEM((cols, 6 * bs), jnp.bfloat16)]
        + [pltpu.SemaphoreType.DMA((n,)) for n in (blocks, blocks // 2)],
        limit=20,
    )(edge, front.reshape(blocks, bs, cols), solved, head, *early)


def run_late_sums(flags, recv, wait):
    chips, bs, _ = recv.shape
    step = 32

    def late_sums(flags, recv, wait, sib):
        def one(i, carry):
            sr, here = i // (bs // step), pl.ds(pl.multiple_of(i % (bs // step) * step, step), step)
            for scp in range(4):
                sums = add_blocks(flags, recv, sr, scp, here, (1,))
                for up in range(2):
                    sib[up, sr, scp, here] = sums[up, 1]
            return carry

        lax.fori_loop(0, 4 * (bs // step), one, 0)

    return call(
        late_sums, shape(2, 4, 4, bs, bs), [SMEM, VMEM, VMEM], VMEM, "late_sums", 96 * bs * bs * 4,
    )(flags, recv, wait)


def run_add_own(core, flags, rest, recv):
    bs, step = recv.shape[1], 32

    def add_own(core, flags, rest, recv, out):
        def one(i, carry):
            sr, here = i // (bs // step), pl.ds(pl.multiple_of(i % (bs // step) * step, step), step)
            for scp in range(4):
                sums = add_blocks(flags, recv, sr, scp, here, (0,))
                for up in range(2):
                    n = 4 * up + sr
                    for lanes, add in zip(pair(scp, bs), spread(core[0] == 0, sums[up, 0], 0.0)):
                        out[n, here, lanes] = rest[n, here, lanes] + add
            return carry

        lax.fori_loop(0, 4 * (bs // step), one, 0)

    return call(
        add_own, shape(*rest.shape), [SMEM, SMEM, VMEM, VMEM], VMEM, "add_own", rest.size * 12, aliases={2: 0},
    )(core, flags, rest, recv)


def run_add_late(core, out, rest, sib):
    blocks, bs, cols = rest.shape
    step = 32

    def add_late(core, before, rest, sib, out, done, sems):
        def write(i):
            return pltpu.make_async_copy(done.at[i], out.at[i, pl.ds(bs, bs)], sems.at[i])

        def one(i, carry):
            up, sr = i // 4, i % 4
            for at in range(0, bs, step):
                here = slice(at, at + step)
                for scp in range(4):
                    for lanes, add in zip(pair(scp, bs), spread(core[0] == 0, 0.0, sib[up, sr, scp, here])):
                        done[i, here, lanes] = rest[i, here, lanes] + add
            write(i).start()
            return carry

        lax.fori_loop(0, blocks, one, 0)
        lax.fori_loop(0, blocks, lambda i, c: (write(i).wait(), c)[1], 0)

    return call(
        add_late, shape(*out.shape), [SMEM, HBM, VMEM, VMEM], HBM, "add_late", out.size * 6,
        [pltpu.VMEM((blocks, bs, cols), F32), pltpu.SemaphoreType.DMA((blocks,))], aliases={1: 0},
    )(core, out, rest, sib)


def body(front, updates, child_map):
    rows_dev, cols_dev = front.shape
    bs = rows_dev // 16
    half = bs // 2
    y, zh, x, zl, t = (lax.axis_index(a) for a in ALL)
    ji, jc = 2 * y + zh, 2 * x + zl
    col = 2 * jc + t
    core = t.reshape(1).astype(jnp.int32)
    blocks = updates.reshape(16, bs, cols_dev)

    def swap(a):
        return lax.ppermute(a, "core", CORE_SWAP)

    def send(load):
        return lax.all_to_all(load, CHIP, 0, 0, tiled=True)

    bits = (child_map.reshape(4, 8, 8) // 8) % 2
    col_bits = lax.dynamic_index_in_dim(bits, jc, 2, keepdims=False).reshape(4, 4, 2)
    col_bits = lax.dynamic_index_in_dim(col_bits, t, 2, keepdims=False)
    row_bits = lax.dynamic_index_in_dim(bits, ji, 2, keepdims=False).reshape(4, 4, 2)
    in_panel = (col == 0) & (jnp.arange(4) == 0)
    side = jnp.stack([(col_bits == t) & ~in_panel, col_bits != t], -1)
    up = row_bits[..., None] == jnp.arange(2)
    flags = [
        (up[:, :, gi, None, :, None] & side[:, None, :, None, :]).astype(F32).reshape(-1) for gi in range(2)
    ]
    live = bits[:, 0, 0] == 0
    marks = (bits.reshape(4, 4, 16).transpose(1, 0, 2) == jnp.arange(2)[:, None, None, None]) & live[:, None]
    marks = jnp.broadcast_to(marks.astype(F32)[..., None], (2, 4, 4, 16, bs))

    low, high, lifted = run_lift(updates, front, bs)
    other = lax.ppermute(high, ALL, [((r * 8 + q) * 2, (r * 8 + q) * 2 + 1) for r in range(8) for q in (0, 4)])
    load0, sent0 = run_put_rows(run_pack(blocks, lifted, 0, 0, half, 32), low, other, core, half)
    recv0 = send(load0)

    load1, sent1 = run_sum_rows(marks, recv0, run_pack(blocks, sent0, 0, half, half, 40), half, half)
    recv1 = send(load1)
    own0, sib0, summed0 = run_child_sums(flags[0], recv0, sent1, half, bs)
    sib0 = swap(sib0)

    recv2 = send(run_pack(blocks, summed0, 1, 0, bs, 0))
    recv2 = pltpu.with_memory_space_constraint(recv2, pltpu.VMEM)

    slabs, corner, own1, sib1 = run_assemble(core, flags[0], recv1, swap(recv1[:, half:]), half)
    sib1 = swap(sib1)
    head = jnp.linalg.cholesky(corner)
    solved = lax.linalg.triangular_solve(
        head, slabs.reshape(24 * bs, bs), left_side=False, lower=True, transpose_a=True
    )
    edge = jnp.stack([ji == 0, col == 0, t == 1]).astype(jnp.int32)
    out, rest, based = run_base(edge, front, solved, head, (own0, sib0, own1, sib1), bs)

    sib2 = swap(run_late_sums(flags[1], recv2, based))
    rest = run_add_own(core, flags[1], rest, recv2)
    return run_add_late(core, out, rest, sib2).reshape(rows_dev, cols_dev)


def solution(mesh):
    fine = Mesh(mesh.devices.reshape(4, 2, 4, 2, 2), ALL)
    spec = P(("y", "zh"), ("x", "zl", "core"))
    return jax.shard_map(body, mesh=fine, in_specs=(spec, spec, P()), out_specs=spec, check_vma=False)
```

```python
import jax
import jax.numpy as jnp
from jax import lax
from jax.experimental import pallas as pl
from jax.experimental.pallas import tpu as pltpu
from jax.sharding import Mesh
from jax.sharding import PartitionSpec as P

CHIP = ("y", "zh", "x", "zl")
ALL = CHIP + ("core",)
CORE_SWAP = [(0, 1), (1, 0)]
VMEM = pl.BlockSpec(memory_space=pltpu.VMEM)
SMEM = pl.BlockSpec(memory_space=pltpu.SMEM)
HBM = pl.BlockSpec(memory_space=pltpu.HBM)
F32 = jnp.float32


def call(kernel, out_shape, in_specs, out_specs, name, moved, scratch=(), aliases=None, limit=16):
    many = isinstance(out_shape, tuple)
    outs = zip(out_shape, out_specs) if many else ((out_shape, out_specs),)
    outs = tuple(pltpu.HBM(array.shape, array.dtype) if spec is HBM else array for array, spec in outs)
    run = pl.pallas_call(
        kernel,
        out_shape=outs if many else outs[0],
        in_specs=in_specs,
        out_specs=out_specs,
        scratch_shapes=scratch,
        input_output_aliases=aliases or {},
        compiler_params=pltpu.CompilerParams(vmem_limit_bytes=limit << 20),
        cost_estimate=pl.CostEstimate(flops=0, bytes_accessed=moved, transcendentals=0),
        name=name,
    )

    def placed(*args):
        return run(*(
            pltpu.with_memory_space_constraint(arg, pltpu.HBM) if spec is HBM else arg
            for arg, spec in zip(args, in_specs)
        ))

    return placed


def shape(*dims):
    return jax.ShapeDtypeStruct(dims, F32)


TOKEN = shape(8, 128)


def run_lift(updates, front, bs):
    rows = updates.shape[0]
    half = bs // 2

    def lift(updates, front, low, high, token, ucol, fcol, sems):
        copies = [
            pltpu.make_async_copy(whole.at[:, pl.ds(0, bs)], part, sems.at[i])
            for i, (whole, part) in enumerate(((updates, ucol), (front, fcol)))
        ]
        for copy in copies:
            copy.start()
        token[...] = jnp.zeros_like(token)
        for at, (copy, part) in enumerate(zip(copies, (ucol, fcol))):
            copy.wait()

            def one(chip, carry):
                low[chip, 16 * at:16 * at + 16] = part[pl.ds(chip, 16, stride=bs), :]
                high[chip, 16 * at:16 * at + 16] = part[pl.ds(half + chip, 16, stride=bs), :]
                return carry

            lax.fori_loop(0, half, one, 0, unroll=8)

    share = shape(half, 32, bs)
    return call(
        lift, (share, share, TOKEN), [HBM, HBM], (VMEM,) * 3, "lift", 16 * rows * bs,
        [pltpu.VMEM((rows, bs), F32), pltpu.VMEM((rows, bs), F32), pltpu.SemaphoreType.DMA((2,))],
    )(updates, front)


def run_pack(blocks, wait, gi, at, rows, extra, ends=False):
    bs = blocks.shape[1]

    def pack(blocks, wait, out, *rest):
        held, read_sems, write_sems, end_sem = rest[-4:]

        def read(j):
            return pltpu.make_async_copy(blocks.at[8 * gi + j, pl.ds(at, rows)], held.at[j], read_sems.at[j])

        def write(j, jc):
            lanes = pl.ds(jc * bs, bs)
            return pltpu.make_async_copy(
                held.at[j, :, lanes], out.at[8 * j + jc, pl.ds(0, rows)], write_sems.at[8 * j + jc]
            )

        for j in range(8):
            read(j).start()
        if ends:
            last = pltpu.make_async_copy(blocks.at[pl.ds(0, 8), pl.ds(bs - 8, 8)], rest[0], end_sem)
            last.start()
        for j in range(8):
            read(j).wait()
            for jc in range(8):
                write(j, jc).start()
        if ends:
            last.wait()
        for j in range(8):
            for jc in range(8):
                write(j, jc).wait()

    load = shape(64, rows + extra, bs)
    return call(
        pack, (load, shape(8, 8, 8 * bs)) if ends else load, [HBM, VMEM], (HBM, VMEM) if ends else HBM, "pack",
        512 * rows * bs,
        [
            pltpu.VMEM((8, rows, 8 * bs), F32), pltpu.SemaphoreType.DMA((8,)), pltpu.SemaphoreType.DMA((64,)),
            pltpu.SemaphoreType.DMA,
        ],
    )(blocks, wait)


def run_put_rows(child_map, ends, load, low, other, rows):
    bs = low.shape[-1]

    def put_rows(child_map, ends, load, low, other, out, token, region, sem):
        y, zh, x, zl, t = (lax.axis_index(a) for a in ALL)
        me, col_pair = 2 * y + zh, 2 * x + zl
        token[...] = jnp.zeros_like(token)
        for c, part in ((0, low), (1, other)):
            @pl.when(t == c)
            def _():
                region[...] = part[...]

        @pl.when((col_pair == 0) & (child_map[me // 4, 0] // 8 % 2 == 0))
        def _():
            for gi in range(2):
                group = 2 * (me % 4) + gi
                up = child_map[me // 4, 8 * group + me] // 8 % 2
                to, of = pl.ds(16 + 8 * up + group, 1), pl.ds(8 * gi + me, 1)
                for at in range(64):
                    region[at, to, :] += region[at, of, :]

        slot = pl.ds(jnp.where(col_pair == 4, slot_of(0, 4), slot_of(me, 0)), 1)
        for j in range(8):
            for jc in range(8):
                region[8 * j + jc, slot, :] = ends[j, 7:8, jc * bs:(jc + 1) * bs]
        copy = pltpu.make_async_copy(region, out.at[:, pl.ds(rows, 32)], sem)
        copy.start()
        copy.wait()

    return call(
        put_rows, (shape(*load.shape), TOKEN), [SMEM, VMEM, HBM, VMEM, VMEM], (HBM, VMEM), "put_rows", 8 * other.size,
        [pltpu.VMEM(low.shape, F32), pltpu.SemaphoreType.DMA], aliases={2: 0},
    )(child_map, ends, load, low, other)


def run_sum_rows(marks, recv, ends, load, first):
    bs = recv.shape[-1]
    last = load.shape[1] - 40

    def sum_rows(marks, recv, ends, load, out, token, kids, total, rows, sems):
        token[...] = jnp.zeros_like(token)
        for up in range(2):
            for sr in range(4):
                acc = jnp.zeros((16, bs), F32)
                for h in range(2):
                    for v in range(2):
                        acc += marks[up, sr, 2 * v + h] * recv[(4 * h + sr) * 8 + 4 * v, first:first + 16]
                kids[pl.ds((up * 4 + sr) * 16, 16)] = acc
        for j in range(8):
            total[j] = kids[pl.ds(j, 16, stride=8), :] + recv[8 * j, first + 16:first + 32]
        copies = []
        for j in range(8):
            for jc in range(8):
                at = 8 * j + jc
                rows[at, 0:8] = ends[j, :, jc * bs:(jc + 1) * bs]
                rows[at, 7:8] = total[0, 0:1]
                rows[at, 8:24] = total[j]
                rows[at, 24:40] = total[jc]
            some = pl.ds(8 * j, 8)
            copies.append(pltpu.make_async_copy(rows.at[some], out.at[some, pl.ds(last, 40)], sems.at[j]))
            copies[-1].start()
        for copy in copies:
            copy.wait()

    return call(
        sum_rows, (shape(*load.shape), TOKEN), [VMEM, VMEM, VMEM, HBM], (HBM, VMEM), "sum_rows", 64 * 40 * bs * 8,
        [
            pltpu.VMEM((128, bs), F32), pltpu.VMEM((8, 16, bs), F32), pltpu.VMEM((64, 40, bs), F32),
            pltpu.SemaphoreType.DMA((8,)),
        ],
        aliases={3: 0},
    )(marks, recv, ends, load)


def add_blocks(flags, recv, sr, scp, here, sides, behind=None):
    sums = {}
    for h in range(2):
        for v in range(2):
            source, col_pair = 4 * h + sr, 4 * v + scp
            rows = here if behind is None else pl.ds(behind + slot_of(source, col_pair), 1)
            block = recv[source * 8 + col_pair, rows]
            for up in range(2):
                for side in sides:
                    term = flags[((((h + 2 * v) * 4 + sr) * 4 + scp) * 2 + up) * 2 + side] * block
                    sums[up, side] = sums[up, side] + term if (up, side) in sums else term
    return sums


def slot_of(row, col_pair):
    return 16 if col_pair == 4 else 8 + row


def child_sums(flags, recv, outs, held, sems, rows):
    step = 32
    more = held[0].shape[3] > rows

    def write(side, sr):
        return pltpu.make_async_copy(held[side].at[:, sr], outs[side].at[:, sr], sems.at[side, sr])

    for sr in range(4):
        def one(i, carry):
            at = pl.multiple_of(i * step, step)
            for scp in range(4):
                sums = add_blocks(flags, recv, sr, scp, pl.ds(at, step), (0, 1))
                for up in range(2):
                    for side in range(2):
                        held[side][up, sr, scp, pl.ds(at, step)] = sums[up, side]
            return carry

        lax.fori_loop(0, rows // step, one, 0)
        for scp in range(4) if more else ():
            sums = add_blocks(flags, recv, sr, scp, None, (0, 1), rows)
            for up in range(2):
                for side in range(2):
                    held[side][up, sr, scp, rows:rows + 1] = sums[up, side]
        for side in range(2):
            write(side, sr).start()

    def finish():
        for sr in range(4):
            for side in range(2):
                write(side, sr).wait()

    return finish


def sums_scratch(rows, bs):
    return [pltpu.VMEM((2, 4, 4, rows, bs), F32)] * 2 + [pltpu.SemaphoreType.DMA((2, 4))]


def run_child_sums(flags, recv, wait, rows, bs):
    def kernel(flags, recv, wait, own, sib, token, *held):
        token[...] = jnp.zeros_like(token)
        child_sums(flags, recv, (own, sib), held[:2], held[2], rows)()

    part = shape(2, 4, 4, rows + 8, bs)
    return call(
        kernel, (part, part, TOKEN), [SMEM, VMEM, VMEM], (HBM, HBM, VMEM), "child_sums", 64 * rows * bs * 8,
        sums_scratch(rows + 8, bs),
    )(flags, recv, wait)


def run_assemble(core, flags, mine, other, first):
    chips, width, bs = mine.shape
    half = bs // 2

    def assemble(core, flags, flat, mine, other, slabs, corner, own, sib, out, sem, *held):
        t = core[0]
        finish = child_sums(flags, mine, (own, sib), held[:2], held[2], first)
        for who, (part, span, at) in enumerate(((flat, width, first), (other, 40, 8))):
            rows_at = pl.multiple_of(half * (t if who == 0 else 1 - t), half)
            for s in range(25):
                start = at + s if s < 16 else at + s + 8 * t if s < 24 else at - 1
                rows = part[pl.ds(start, half, stride=span), :]
                if s < 24:
                    out[s, pl.ds(rows_at, half)] = rows
                else:
                    corner[pl.ds(rows_at, half)] = rows
        copy = pltpu.make_async_copy(out, slabs, sem)
        copy.start()
        finish()
        copy.wait()

    part = shape(2, 4, 4, first, bs)
    return call(
        assemble, (shape(24, bs, bs), shape(bs, bs), part, part), [SMEM, SMEM, VMEM, VMEM, VMEM], (HBM, VMEM, HBM, HBM),
        "assemble", 200 * bs * bs,
        [pltpu.VMEM((24, bs, bs), F32), pltpu.SemaphoreType.DMA] + sums_scratch(first, bs),
    )(core, flags, mine.reshape(chips * width, bs), mine, other.reshape(chips * 40, bs))


def split(a):
    high = a.astype(jnp.bfloat16)
    left = a - high.astype(F32)
    mid = left.astype(jnp.bfloat16)
    return high, mid, (left - mid.astype(F32)).astype(jnp.bfloat16)


def spread(left, mine, other):
    return jnp.where(left, mine, other), jnp.where(left, other, mine)


def pair(scp, bs):
    return slice(2 * scp * bs, (2 * scp + 1) * bs), slice((2 * scp + 1) * bs, (2 * scp + 2) * bs)


def run_base(edge, front, solved, head, early, bs):
    rows, cols = front.shape
    blocks, tile, step = rows // bs, 256, 32
    cut = early[0].shape[3] - 8

    group = 4

    def base(edge, front, solved, head, own0, sib0, own1, sib1, out, rest, token, held, right, o0, s0, o1, s1, sems, more, back):
        top, col_zero, left = edge[0] == 1, edge[1] == 1, edge[2] == 0
        token[...] = jnp.zeros_like(token)

        def read(i):
            return pltpu.make_async_copy(front.at[i], held.at[i], sems.at[i])

        def write(i, to):
            return pltpu.make_async_copy(held.at[i], to.at[i // 2, pl.ds(0, bs)], back.at[i])

        sums = [
            pltpu.make_async_copy(src, dst, more.at[n])
            for n, (src, dst) in enumerate(((own0, o0), (sib0, s0), (own1, o1), (sib1, s1)))
        ]
        for i in range(blocks):
            read(i).start()
            if i == group - 1:
                for copy in sums:
                    copy.start()

        for at in range(0, cols, bs):
            high, mid, low = split(solved[rows + at:rows + at + bs])
            right[at:at + bs] = jnp.concatenate([high, high, mid, high, mid, low], axis=1)

        def some(q, carry):
            own = solved[pl.ds(pl.multiple_of(q * group * bs, group * bs), group * bs)]
            high, mid, low = split(own)
            parts = jnp.concatenate([high, mid, high, low, mid, high], axis=1)
            for n in range(group):
                read(q * group + n).wait()
            for at in range(0, cols, tile):
                lanes = slice(at, at + tile)
                product = lax.dot_general(
                    parts, right[at:at + tile], (((1,), (1,)), ((), ())), preferred_element_type=F32
                )
                for n in range(group):
                    keep = jnp.where(top & (q == 0), 0.0, 1.0) if n == 0 else 1.0
                    held[q * group + n, :, lanes] -= keep * product[n * bs:(n + 1) * bs]

            @pl.when(col_zero)
            def _():
                for n in range(group):
                    held[q * group + n, :, 0:bs] = own[n * bs:(n + 1) * bs]

            @pl.when(top & col_zero & (q == 0))
            def _():
                held[0, :, 0:bs] = head[...]

            @pl.when(q == 0)
            def _():
                for copy in sums:
                    copy.wait()
                for late, soon in ((o1, o0), (s1, s0)):
                    late[:, :, :, bs - cut - 1:bs - cut] = soon[:, :, :, cut:cut + 1]

            for n in range(0, group, 2):
                i = q * group + n
                up, sr = i // 8, i // 2 % 4
                for at in range(0, bs, step):
                    here = slice(at, at + step)
                    own, sib, inner = (o0, s0, at) if at < cut else (o1, s1, at - cut)
                    for scp in range(4):
                        two = spread(left, own[up, sr, scp, inner:inner + step], sib[up, sr, scp, inner:inner + step])
                        for lanes, add in zip(pair(scp, bs), two):
                            held[i, here, lanes] += add
                write(i, out).start()
                write(i + 1, rest).start()
            return carry

        lax.fori_loop(0, blocks // group, some, 0)

        def finish(n, carry):
            write(2 * n, out).wait()
            write(2 * n + 1, rest).wait()
            return carry

        lax.fori_loop(0, blocks // 2, finish, 0)

    parts = [pltpu.VMEM(a.shape, F32) for a in early]
    return call(
        base, (shape(blocks // 2, 2 * bs, cols), shape(blocks // 2, bs, cols), TOKEN), [SMEM, HBM, VMEM, VMEM] + [HBM] * 4,
        (HBM, HBM, VMEM), "base", rows * cols * 8,
        [pltpu.VMEM((blocks, bs, cols), F32), pltpu.VMEM((cols, 6 * bs), jnp.bfloat16)] + parts
        + [pltpu.SemaphoreType.DMA((n,)) for n in (blocks, 4, blocks)],
        limit=28,
    )(edge, front.reshape(blocks, bs, cols), solved, head, *early)


def run_late_sums(flags, recv, wait):
    chips, bs, _ = recv.shape
    step = 32

    def late_sums(flags, recv, wait, sib, held, sems):
        def read(sr, h):
            some = pl.ds((4 * h + sr) * 8, 8)
            return pltpu.make_async_copy(recv.at[some], held.at[some], sems.at[2 * sr + h])

        for sr in range(4):
            for h in range(2):
                read(sr, h).start()
        for sr in range(4):
            for h in range(2):
                read(sr, h).wait()

            def one(i, carry):
                here = pl.ds(pl.multiple_of(i * step, step), step)
                for scp in range(4):
                    sums = add_blocks(flags, held, sr, scp, here, (1,))
                    for up in range(2):
                        sib[up, sr, scp, here] = sums[up, 1]
                return carry

            lax.fori_loop(0, bs // step, one, 0)

    return call(
        late_sums, shape(2, 4, 4, bs, bs), [SMEM, HBM, VMEM], VMEM, "late_sums", 96 * bs * bs * 4,
        [pltpu.VMEM((chips, bs, bs), F32), pltpu.SemaphoreType.DMA((8,))],
    )(flags, recv, wait)


def run_add_own(core, flags, rest, recv):
    blocks, bs, cols = rest.shape
    step = 32

    def add_own(core, flags, rest, recv, out, held, sems, more):
        def read(sr, h):
            some = pl.ds((4 * h + sr) * 8, 8)
            return pltpu.make_async_copy(recv.at[some], held.at[some], sems.at[2 * sr + h])

        def base(i):
            return pltpu.make_async_copy(rest.at[i], out.at[i], more.at[i])

        for sr in range(4):
            for n in range(2):
                read(sr, n).start()
                base(4 * n + sr).start()
        for sr in range(4):
            for n in range(2):
                read(sr, n).wait()
                base(4 * n + sr).wait()

            def one(i, carry):
                here = pl.ds(pl.multiple_of(i * step, step), step)
                for scp in range(4):
                    sums = add_blocks(flags, held, sr, scp, here, (0,))
                    for up in range(2):
                        two = spread(core[0] == 0, sums[up, 0], 0.0)
                        for lanes, add in zip(pair(scp, bs), two):
                            out[4 * up + sr, here, lanes] += add
                return carry

            lax.fori_loop(0, bs // step, one, 0)

    return call(
        add_own, shape(blocks, bs, cols), [SMEM, SMEM, HBM, HBM], VMEM, "add_own", blocks * bs * cols * 12,
        [pltpu.VMEM(recv.shape, F32), pltpu.SemaphoreType.DMA((8,)), pltpu.SemaphoreType.DMA((8,))],
    )(core, flags, rest, recv)


def run_add_late(core, out, rest, sib):
    blocks, bs, cols = rest.shape
    step = 32

    def add_late(core, before, rest, sib, out, done, sems):
        def write(i):
            return pltpu.make_async_copy(done.at[i], out.at[i, pl.ds(bs, bs)], sems.at[i])

        def one(i, carry):
            up, sr = i // 4, i % 4
            for at in range(0, bs, step):
                here = slice(at, at + step)
                for scp in range(4):
                    for lanes, add in zip(pair(scp, bs), spread(core[0] == 0, 0.0, sib[up, sr, scp, here])):
                        done[i, here, lanes] = rest[i, here, lanes] + add
            write(i).start()
            return carry

        lax.fori_loop(0, blocks, one, 0)
        lax.fori_loop(0, blocks, lambda i, c: (write(i).wait(), c)[1], 0)

    return call(
        add_late, shape(*out.shape), [SMEM, HBM, VMEM, VMEM], HBM, "add_late", out.size * 6,
        [pltpu.VMEM((blocks, bs, cols), F32), pltpu.SemaphoreType.DMA((blocks,))], aliases={1: 0},
    )(core, out, rest, sib)


def body(front, updates, child_map):
    rows_dev, cols_dev = front.shape
    bs = rows_dev // 16
    half = bs // 2
    y, zh, x, zl, t = (lax.axis_index(a) for a in ALL)
    ji, jc = 2 * y + zh, 2 * x + zl
    col = 2 * jc + t
    core = t.reshape(1).astype(jnp.int32)
    blocks = updates.reshape(16, bs, cols_dev)

    def swap(a):
        return lax.ppermute(a, "core", CORE_SWAP)

    def send(load):
        return lax.all_to_all(load, CHIP, 0, 0, tiled=True)

    bits = (child_map.reshape(4, 8, 8) // 8) % 2
    col_bits = lax.dynamic_index_in_dim(bits, jc, 2, keepdims=False).reshape(4, 4, 2)
    col_bits = lax.dynamic_index_in_dim(col_bits, t, 2, keepdims=False)
    row_bits = lax.dynamic_index_in_dim(bits, ji, 2, keepdims=False).reshape(4, 4, 2)
    in_panel = (col == 0) & (jnp.arange(4) == 0)
    side = jnp.stack([(col_bits == t) & ~in_panel, col_bits != t], -1)
    up = row_bits[..., None] == jnp.arange(2)
    flags = [
        (up[:, :, gi, None, :, None] & side[:, None, :, None, :]).astype(F32).reshape(-1) for gi in range(2)
    ]
    live = bits[:, 0, 0] == 0
    marks = (bits.reshape(4, 4, 16).transpose(1, 0, 2) == jnp.arange(2)[:, None, None, None]) & live[:, None]
    sr_at, h_at, j_at = jnp.arange(4)[:, None, None], jnp.arange(4)[None, :, None], jnp.arange(16)[None, None] % 8
    marks &= ~((h_at < 2) & (4 * h_at + sr_at == j_at))
    marks = jnp.broadcast_to(marks.astype(F32)[..., None], (2, 4, 4, 16, bs))

    low, high, lifted = run_lift(updates, front, bs)
    other = lax.ppermute(high, ALL, [((r * 8 + q) * 2, (r * 8 + q) * 2 + 1) for r in range(8) for q in (0, 4)])
    load0, ends = run_pack(blocks, lifted, 0, 0, half, 32, True)
    load0, sent0 = run_put_rows(child_map, ends, load0, low, other, half)
    recv0 = send(load0)

    load1, sent1 = run_sum_rows(marks, recv0, ends, run_pack(blocks, sent0, 0, half, half, 32), half)
    recv1 = send(load1)
    own0, sib0, summed0 = run_child_sums(flags[0], recv0, sent1, half, bs)
    sib0 = swap(sib0)

    recv2 = send(run_pack(blocks, summed0, 1, 0, bs, 0))

    slabs, corner, own1, sib1 = run_assemble(core, flags[0], recv1, swap(recv1[:, half - 8:]), half)
    sib1 = swap(sib1)
    head = jnp.linalg.cholesky(corner)
    solved = lax.linalg.triangular_solve(
        head, slabs.reshape(24 * bs, bs), left_side=False, lower=True, transpose_a=True
    )
    edge = jnp.stack([ji == 0, col == 0, t == 1]).astype(jnp.int32)
    out, rest, based = run_base(edge, front, solved, head, (own0, sib0, own1, sib1), bs)

    sib2 = swap(run_late_sums(flags[1], recv2, based))
    rest = run_add_own(core, flags[1], rest, recv2)
    return run_add_late(core, out, rest, sib2).reshape(rows_dev, cols_dev)


def solution(mesh):
    fine = Mesh(mesh.devices.reshape(4, 2, 4, 2, 2), ALL)
    spec = P(("y", "zh"), ("x", "zl", "core"))
    return jax.shard_map(body, mesh=fine, in_specs=(spec, spec, P()), out_specs=spec, check_vma=False)
```

```python
import jax
import jax.numpy as jnp
from jax import lax
from jax.experimental import pallas as pl
from jax.experimental.pallas import tpu as pltpu
from jax.sharding import Mesh
from jax.sharding import PartitionSpec as P

CHIP = ("y", "zh", "x", "zl")
ALL = CHIP + ("core",)
CORE_SWAP = [(0, 1), (1, 0)]
VMEM = pl.BlockSpec(memory_space=pltpu.VMEM)
SMEM = pl.BlockSpec(memory_space=pltpu.SMEM)
HBM = pl.BlockSpec(memory_space=pltpu.HBM)
F32 = jnp.float32


def call(kernel, out_shape, in_specs, out_specs, name, moved, scratch=(), aliases=None, limit=16):
    many = isinstance(out_shape, tuple)
    outs = zip(out_shape, out_specs) if many else ((out_shape, out_specs),)
    outs = tuple(pltpu.HBM(array.shape, array.dtype) if spec is HBM else array for array, spec in outs)
    run = pl.pallas_call(
        kernel,
        out_shape=outs if many else outs[0],
        in_specs=in_specs,
        out_specs=out_specs,
        scratch_shapes=scratch,
        input_output_aliases=aliases or {},
        compiler_params=pltpu.CompilerParams(vmem_limit_bytes=limit << 20),
        cost_estimate=pl.CostEstimate(flops=0, bytes_accessed=moved, transcendentals=0),
        name=name,
    )

    def placed(*args):
        return run(*(
            pltpu.with_memory_space_constraint(arg, pltpu.HBM) if spec is HBM else arg
            for arg, spec in zip(args, in_specs)
        ))

    return placed


def shape(*dims):
    return jax.ShapeDtypeStruct(dims, F32)


TOKEN = shape(8, 128)


def run_lift(updates, front, bs):
    rows = updates.shape[0]
    half = bs // 2

    cuts = 4
    some = half // cuts

    def lift(updates, front, low, high, token, ucol, fcol, sems):
        def read(i, cut, core):
            whole, part = ((updates, ucol), (front, fcol))[i]
            here = pl.ds(core * half + cut * some, some)
            return pltpu.make_async_copy(
                whole.at[:, here, pl.ds(0, bs)], part.reshape(17, bs, bs).at[pl.ds(0, 16), here], sems.at[i, cut, core]
            )

        pieces = [(i, cut, core) for cut in range(cuts) for i in range(2) for core in range(2)]
        for piece in pieces:
            read(*piece).start()
        token[...] = jnp.zeros_like(token)
        for i, cut, core in pieces:
            read(i, cut, core).wait()
            part, out = (ucol, fcol)[i], (low, high)[core]

            def one(n, carry):
                chip = cut * some + n
                out[chip, 16 * i:16 * i + 16] = part[pl.ds(core * half + chip, 16, stride=bs), :]
                return carry

            lax.fori_loop(0, some, one, 0, unroll=8)

    share = shape(half, 32, bs)
    blocks = (16, bs, updates.shape[1])
    return call(
        lift, (share, share, TOKEN), [HBM, HBM], (VMEM,) * 3, "lift", 16 * rows * bs,
        [pltpu.VMEM((rows + bs, bs), F32)] * 2 + [pltpu.SemaphoreType.DMA((2, cuts, 2))],
    )(updates.reshape(blocks), front.reshape(blocks))


def run_pack(blocks, wait, gi, at, rows, extra, ends=False):
    bs = blocks.shape[1]

    def pack(blocks, wait, out, *rest):
        held, read_sems, write_sems, end_sem = rest[-4:]

        def read(j):
            return pltpu.make_async_copy(blocks.at[8 * gi + j, pl.ds(at, rows)], held.at[j], read_sems.at[j])

        def write(j, jc):
            lanes = pl.ds(jc * bs, bs)
            return pltpu.make_async_copy(
                held.at[j, :, lanes], out.at[8 * j + jc, pl.ds(0, rows)], write_sems.at[8 * j + jc]
            )

        for j in range(8):
            read(j).start()
        if ends:
            last = pltpu.make_async_copy(blocks.at[pl.ds(0, 8), pl.ds(bs - 8, 8)], rest[0], end_sem)
            last.start()
        for j in range(8):
            read(j).wait()
            for jc in range(8):
                write(j, jc).start()
        if ends:
            last.wait()
        for j in range(8):
            for jc in range(8):
                write(j, jc).wait()

    load = shape(64, rows + extra, bs)
    return call(
        pack, (load, shape(8, 8, 8 * bs)) if ends else load, [HBM, VMEM], (HBM, VMEM) if ends else HBM, "pack",
        512 * rows * bs,
        [
            pltpu.VMEM((8, rows, 8 * bs), F32), pltpu.SemaphoreType.DMA((8,)), pltpu.SemaphoreType.DMA((64,)),
            pltpu.SemaphoreType.DMA,
        ],
    )(blocks, wait)


def run_put_rows(child_map, ends, load, low, other, rows):
    bs = low.shape[-1]

    def put_rows(child_map, ends, load, low, other, out, token, region, sems):
        y, zh, x, zl, t = (lax.axis_index(a) for a in ALL)
        me, col_pair = 2 * y + zh, 2 * x + zl
        token[...] = jnp.zeros_like(token)
        for c, part in ((0, low), (1, other)):
            @pl.when(t == c)
            def _():
                region[...] = part[...]

        adds = (col_pair == 0) & (child_map[me // 4, 0] // 8 % 2 == 0)
        slot = pl.ds(jnp.where(col_pair == 4, slot_of(0, 4), slot_of(me, 0)), 1)
        copies = []
        for j in range(8):
            @pl.when(adds)
            def _():
                for gi in range(2):
                    group = 2 * (me % 4) + gi
                    up = child_map[me // 4, 8 * group + me] // 8 % 2
                    to, of = pl.ds(16 + 8 * up + group, 1), pl.ds(8 * gi + me, 1)
                    for at in range(8 * j, 8 * j + 8):
                        region[at, to, :] += region[at, of, :]

            for jc in range(8):
                region[8 * j + jc, slot, :] = ends[j, 7:8, jc * bs:(jc + 1) * bs]
            some = pl.ds(8 * j, 8)
            copies.append(pltpu.make_async_copy(region.at[some], out.at[some, pl.ds(rows, 32)], sems.at[j]))
            copies[-1].start()
        for copy in copies:
            copy.wait()

    return call(
        put_rows, (shape(*load.shape), TOKEN), [SMEM, VMEM, HBM, VMEM, VMEM], (HBM, VMEM), "put_rows", 8 * other.size,
        [pltpu.VMEM(low.shape, F32), pltpu.SemaphoreType.DMA((8,))], aliases={2: 0},
    )(child_map, ends, load, low, other)


def run_sum_rows(marks, recv, ends, load, first):
    bs = recv.shape[-1]
    last = load.shape[1] - 40

    def sum_rows(marks, recv, ends, load, out, token, kids, total, rows, sems):
        token[...] = jnp.zeros_like(token)
        for up in range(2):
            for sr in range(4):
                acc = jnp.zeros((16, bs), F32)
                for h in range(2):
                    for v in range(2):
                        acc += marks[up, sr, 2 * v + h] * recv[(4 * h + sr) * 8 + 4 * v, first:first + 16]
                kids[pl.ds((up * 4 + sr) * 16, 16)] = acc
        for j in range(8):
            total[j] = kids[pl.ds(j, 16, stride=8), :] + recv[8 * j, first + 16:first + 32]
        copies = []
        for j in range(8):
            for jc in range(8):
                at = 8 * j + jc
                rows[at, 0:8] = ends[j, :, jc * bs:(jc + 1) * bs]
                rows[at, 7:8] = total[0, 0:1]
                rows[at, 8:24] = total[j]
                rows[at, 24:40] = total[jc]
            some = pl.ds(8 * j, 8)
            copies.append(pltpu.make_async_copy(rows.at[some], out.at[some, pl.ds(last, 40)], sems.at[j]))
            copies[-1].start()
        for copy in copies:
            copy.wait()

    return call(
        sum_rows, (shape(*load.shape), TOKEN), [VMEM, VMEM, VMEM, HBM], (HBM, VMEM), "sum_rows", 64 * 40 * bs * 8,
        [
            pltpu.VMEM((136, bs), F32), pltpu.VMEM((8, 16, bs), F32), pltpu.VMEM((64, 40, bs), F32),
            pltpu.SemaphoreType.DMA((8,)),
        ],
        aliases={3: 0},
    )(marks, recv, ends, load)


def add_blocks(flags, recv, sr, scp, here, sides, behind=None):
    sums = {}
    for h in range(2):
        for v in range(2):
            source, col_pair = 4 * h + sr, 4 * v + scp
            rows = here if behind is None else pl.ds(behind + slot_of(source, col_pair), 1)
            block = recv[source * 8 + col_pair, rows]
            for up in range(2):
                for side in sides:
                    term = flags[((((h + 2 * v) * 4 + sr) * 4 + scp) * 2 + up) * 2 + side] * block
                    sums[up, side] = sums[up, side] + term if (up, side) in sums else term
    return sums


def slot_of(row, col_pair):
    return 16 if col_pair == 4 else 8 + row


def child_sums(flags, recv, outs, held, sems, rows):
    step = 32
    more = held[0].shape[3] > rows

    def write(side, sr):
        return pltpu.make_async_copy(held[side].at[:, sr], outs[side].at[:, sr], sems.at[side, sr])

    for sr in range(4):
        def one(i, carry):
            at = pl.multiple_of(i * step, step)
            for scp in range(4):
                sums = add_blocks(flags, recv, sr, scp, pl.ds(at, step), (0, 1))
                for up in range(2):
                    for side in range(2):
                        held[side][up, sr, scp, pl.ds(at, step)] = sums[up, side]
            return carry

        lax.fori_loop(0, rows // step, one, 0)
        for scp in range(4) if more else ():
            sums = add_blocks(flags, recv, sr, scp, None, (0, 1), rows)
            for up in range(2):
                for side in range(2):
                    held[side][up, sr, scp, rows:rows + 1] = sums[up, side]
        for side in range(2):
            write(side, sr).start()

    def finish():
        for sr in range(4):
            for side in range(2):
                write(side, sr).wait()

    return finish


def sums_scratch(rows, bs):
    return [pltpu.VMEM((2, 4, 4, rows, bs), F32)] * 2 + [pltpu.SemaphoreType.DMA((2, 4))]


def run_child_sums(flags, recv, wait, rows, bs):
    def kernel(flags, recv, wait, own, sib, token, *held):
        token[...] = jnp.zeros_like(token)
        child_sums(flags, recv, (own, sib), held[:2], held[2], rows)()

    part = shape(2, 4, 4, rows + 8, bs)
    return call(
        kernel, (part, part, TOKEN), [SMEM, VMEM, VMEM], (HBM, HBM, VMEM), "child_sums", 64 * rows * bs * 8,
        sums_scratch(rows + 8, bs),
    )(flags, recv, wait)


def run_assemble(core, flags, mine, other, first):
    chips, width, bs = mine.shape
    half = bs // 2

    wide = width - first + 8

    def assemble(core, flags, mine, other, slabs, corner, own, sib, here, there, out, sems, *held):
        t = core[0]
        copies = [
            pltpu.make_async_copy(
                mine.at[:, pl.ds(first - 8, wide)], here.reshape(chips + 1, wide, bs).at[pl.ds(0, chips)], sems.at[0]
            ),
            pltpu.make_async_copy(other, there.reshape(chips + 1, wide, bs).at[pl.ds(0, chips)], sems.at[1]),
        ]
        for copy in copies:
            copy.start()
        finish = child_sums(flags, mine, (own, sib), held[:2], held[2], first)
        for who, (copy, part) in enumerate(zip(copies, (here, there))):
            copy.wait()
            rows_at = pl.multiple_of(half * (t if who == 0 else 1 - t), half)
            for s in range(25):
                start = 8 + s if s < 16 else 8 + s + 8 * t if s < 24 else 7
                rows = part[pl.ds(start, half, stride=wide), :]
                if s < 24:
                    out[s, pl.ds(rows_at, half)] = rows
                else:
                    corner[pl.ds(rows_at, half)] = rows
        copy = pltpu.make_async_copy(out, slabs, sems.at[2])
        copy.start()
        finish()
        copy.wait()

    part = shape(2, 4, 4, first, bs)
    return call(
        assemble, (shape(24, bs, bs), shape(bs, bs), part, part), [SMEM, SMEM, VMEM, HBM], (HBM, VMEM, HBM, HBM),
        "assemble", 200 * bs * bs,
        [pltpu.VMEM(((chips + 1) * wide, bs), F32)] * 2 + [pltpu.VMEM((24, bs, bs), F32), pltpu.SemaphoreType.DMA((3,))]
        + sums_scratch(first, bs),
    )(core, flags, mine, other)


def split(a):
    high = a.astype(jnp.bfloat16)
    left = a - high.astype(F32)
    mid = left.astype(jnp.bfloat16)
    return high, mid, (left - mid.astype(F32)).astype(jnp.bfloat16)


def spread(left, mine, other):
    return jnp.where(left, mine, other), jnp.where(left, other, mine)


def pair(scp, bs):
    return slice(2 * scp * bs, (2 * scp + 1) * bs), slice((2 * scp + 1) * bs, (2 * scp + 2) * bs)


def run_base(edge, front, solved, head, early, bs):
    rows, cols = front.shape
    blocks, tile, step = rows // bs, 256, 32
    cut = early[0].shape[3] - 8

    group = 4

    def base(edge, front, solved, head, own0, sib0, own1, sib1, out, rest, token, held, right, o0, s0, o1, s1, sems, more, back):
        top, col_zero, left = edge[0] == 1, edge[1] == 1, edge[2] == 0
        token[...] = jnp.zeros_like(token)

        def read(i):
            return pltpu.make_async_copy(front.at[i], held.at[i], sems.at[i])

        def write(i, to):
            return pltpu.make_async_copy(held.at[i], to.at[i // 2, pl.ds(0, bs)], back.at[i])

        sums = [
            pltpu.make_async_copy(src, dst, more.at[n])
            for n, (src, dst) in enumerate(((own0, o0), (sib0, s0), (own1, o1), (sib1, s1)))
        ]
        for i in range(blocks):
            read(i).start()
            if i == group - 1:
                for copy in sums:
                    copy.start()

        for at in range(0, cols, bs):
            high, mid, low = split(solved[rows + at:rows + at + bs])
            right[at:at + bs] = jnp.concatenate([high, high, mid, high, mid, low], axis=1)

        def some(q, carry):
            own = solved[pl.ds(pl.multiple_of(q * group * bs, group * bs), group * bs)]
            high, mid, low = split(own)
            parts = jnp.concatenate([high, mid, high, low, mid, high], axis=1)
            for n in range(group):
                read(q * group + n).wait()
            for at in range(0, cols, tile):
                lanes = slice(at, at + tile)
                product = lax.dot_general(
                    parts, right[at:at + tile], (((1,), (1,)), ((), ())), preferred_element_type=F32
                )
                for n in range(group):
                    keep = jnp.where(top & (q == 0), 0.0, 1.0) if n == 0 else 1.0
                    held[q * group + n, :, lanes] -= keep * product[n * bs:(n + 1) * bs]

            @pl.when(col_zero)
            def _():
                for n in range(group):
                    held[q * group + n, :, 0:bs] = own[n * bs:(n + 1) * bs]

            @pl.when(top & col_zero & (q == 0))
            def _():
                held[0, :, 0:bs] = head[...]

            @pl.when(q == 0)
            def _():
                for copy in sums:
                    copy.wait()
                for late, soon in ((o1, o0), (s1, s0)):
                    late[:, :, :, bs - cut - 1:bs - cut] = soon[:, :, :, cut:cut + 1]

            for n in range(0, group, 2):
                i = q * group + n
                up, sr = i // 8, i // 2 % 4
                for at in range(0, bs, step):
                    here = slice(at, at + step)
                    own, sib, inner = (o0, s0, at) if at < cut else (o1, s1, at - cut)
                    for scp in range(4):
                        two = spread(left, own[up, sr, scp, inner:inner + step], sib[up, sr, scp, inner:inner + step])
                        for lanes, add in zip(pair(scp, bs), two):
                            held[i, here, lanes] += add
                write(i, out).start()
                write(i + 1, rest).start()
            return carry

        lax.fori_loop(0, blocks // group, some, 0)

        def finish(n, carry):
            write(2 * n, out).wait()
            write(2 * n + 1, rest).wait()
            return carry

        lax.fori_loop(0, blocks // 2, finish, 0)

    parts = [pltpu.VMEM(a.shape, F32) for a in early]
    return call(
        base, (shape(blocks // 2, 2 * bs, cols), shape(blocks // 2, bs, cols), TOKEN), [SMEM, HBM, VMEM, VMEM] + [HBM] * 4,
        (HBM, HBM, VMEM), "base", rows * cols * 8,
        [pltpu.VMEM((blocks, bs, cols), F32), pltpu.VMEM((cols, 6 * bs), jnp.bfloat16)] + parts
        + [pltpu.SemaphoreType.DMA((n,)) for n in (blocks, 4, blocks)],
        limit=28,
    )(edge, front.reshape(blocks, bs, cols), solved, head, *early)


def run_late_sums(flags, recv, wait):
    chips, bs, _ = recv.shape
    step = 32

    def late_sums(flags, recv, wait, sib, held, sems):
        def read(sr, h):
            some = pl.ds((4 * h + sr) * 8, 8)
            return pltpu.make_async_copy(recv.at[some], held.at[some], sems.at[2 * sr + h])

        for sr in range(4):
            for h in range(2):
                read(sr, h).start()
        for sr in range(4):
            for h in range(2):
                read(sr, h).wait()

            def one(i, carry):
                here = pl.ds(pl.multiple_of(i * step, step), step)
                for scp in range(4):
                    sums = add_blocks(flags, held, sr, scp, here, (1,))
                    for up in range(2):
                        sib[up, sr, scp, here] = sums[up, 1]
                return carry

            lax.fori_loop(0, bs // step, one, 0)

    return call(
        late_sums, shape(2, 4, 4, bs, bs), [SMEM, HBM, VMEM], VMEM, "late_sums", 96 * bs * bs * 4,
        [pltpu.VMEM((chips, bs, bs), F32), pltpu.SemaphoreType.DMA((8,))],
    )(flags, recv, wait)


def run_add_own(core, flags, rest, recv):
    blocks, bs, cols = rest.shape
    step = 32

    def add_own(core, flags, rest, recv, out, held, sems, more):
        def read(sr, h):
            some = pl.ds((4 * h + sr) * 8, 8)
            return pltpu.make_async_copy(recv.at[some], held.at[some], sems.at[2 * sr + h])

        def base(i):
            return pltpu.make_async_copy(rest.at[i], out.at[i], more.at[i])

        for sr in range(4):
            for n in range(2):
                read(sr, n).start()
                base(4 * n + sr).start()
        for sr in range(4):
            for n in range(2):
                read(sr, n).wait()
                base(4 * n + sr).wait()

            def one(i, carry):
                here = pl.ds(pl.multiple_of(i * step, step), step)
                for scp in range(4):
                    sums = add_blocks(flags, held, sr, scp, here, (0,))
                    for up in range(2):
                        two = spread(core[0] == 0, sums[up, 0], 0.0)
                        for lanes, add in zip(pair(scp, bs), two):
                            out[4 * up + sr, here, lanes] += add
                return carry

            lax.fori_loop(0, bs // step, one, 0)

    return call(
        add_own, shape(blocks, bs, cols), [SMEM, SMEM, HBM, HBM], VMEM, "add_own", blocks * bs * cols * 12,
        [pltpu.VMEM(recv.shape, F32), pltpu.SemaphoreType.DMA((8,)), pltpu.SemaphoreType.DMA((8,))],
    )(core, flags, rest, recv)


def run_add_late(core, out, rest, sib):
    blocks, bs, cols = rest.shape
    step = 32

    def add_late(core, before, rest, sib, out, done, sems):
        def write(i):
            return pltpu.make_async_copy(done.at[i], out.at[i, pl.ds(bs, bs)], sems.at[i])

        def one(i, carry):
            up, sr = i // 4, i % 4
            for at in range(0, bs, step):
                here = slice(at, at + step)
                for scp in range(4):
                    for lanes, add in zip(pair(scp, bs), spread(core[0] == 0, 0.0, sib[up, sr, scp, here])):
                        done[i, here, lanes] = rest[i, here, lanes] + add
            write(i).start()
            return carry

        lax.fori_loop(0, blocks, one, 0)
        lax.fori_loop(0, blocks, lambda i, c: (write(i).wait(), c)[1], 0)

    return call(
        add_late, shape(*out.shape), [SMEM, HBM, VMEM, VMEM], HBM, "add_late", out.size * 6,
        [pltpu.VMEM((blocks, bs, cols), F32), pltpu.SemaphoreType.DMA((blocks,))], aliases={1: 0},
    )(core, out, rest, sib)


def body(front, updates, child_map):
    rows_dev, cols_dev = front.shape
    bs = rows_dev // 16
    half = bs // 2
    y, zh, x, zl, t = (lax.axis_index(a) for a in ALL)
    ji, jc = 2 * y + zh, 2 * x + zl
    col = 2 * jc + t
    core = t.reshape(1).astype(jnp.int32)
    blocks = updates.reshape(16, bs, cols_dev)

    def swap(a):
        return lax.ppermute(a, "core", CORE_SWAP)

    def send(load):
        return lax.all_to_all(load, CHIP, 0, 0, tiled=True)

    bits = (child_map.reshape(4, 8, 8) // 8) % 2
    col_bits = lax.dynamic_index_in_dim(bits, jc, 2, keepdims=False).reshape(4, 4, 2)
    col_bits = lax.dynamic_index_in_dim(col_bits, t, 2, keepdims=False)
    row_bits = lax.dynamic_index_in_dim(bits, ji, 2, keepdims=False).reshape(4, 4, 2)
    in_panel = (col == 0) & (jnp.arange(4) == 0)
    side = jnp.stack([(col_bits == t) & ~in_panel, col_bits != t], -1)
    up = row_bits[..., None] == jnp.arange(2)
    flags = [
        (up[:, :, gi, None, :, None] & side[:, None, :, None, :]).astype(F32).reshape(-1) for gi in range(2)
    ]
    live = bits[:, 0, 0] == 0
    marks = (bits.reshape(4, 4, 16).transpose(1, 0, 2) == jnp.arange(2)[:, None, None, None]) & live[:, None]
    sr_at, h_at, j_at = jnp.arange(4)[:, None, None], jnp.arange(4)[None, :, None], jnp.arange(16)[None, None] % 8
    marks &= ~((h_at < 2) & (4 * h_at + sr_at == j_at))
    marks = jnp.broadcast_to(marks.astype(F32)[..., None], (2, 4, 4, 16, bs))

    low, high, lifted = run_lift(updates, front, bs)
    other = lax.ppermute(high, ALL, [((r * 8 + q) * 2, (r * 8 + q) * 2 + 1) for r in range(8) for q in (0, 4)])
    load0, ends = run_pack(blocks, lifted, 0, 0, half, 32, True)
    load0, sent0 = run_put_rows(child_map, ends, load0, low, other, half)
    recv0 = send(load0)

    load1, sent1 = run_sum_rows(marks, recv0, ends, run_pack(blocks, sent0, 0, half, half, 32), half)
    recv1 = send(load1)
    own0, sib0, summed0 = run_child_sums(flags[0], recv0, sent1, half, bs)
    sib0 = swap(sib0)

    recv2 = send(run_pack(blocks, summed0, 1, 0, bs, 0))

    slabs, corner, own1, sib1 = run_assemble(core, flags[0], recv1, swap(recv1[:, half - 8:]), half)
    sib1 = swap(sib1)
    head = jnp.linalg.cholesky(corner)
    solved = lax.linalg.triangular_solve(
        head, slabs.reshape(24 * bs, bs), left_side=False, lower=True, transpose_a=True
    )
    edge = jnp.stack([ji == 0, col == 0, t == 1]).astype(jnp.int32)
    out, rest, based = run_base(edge, front, solved, head, (own0, sib0, own1, sib1), bs)

    sib2 = swap(run_late_sums(flags[1], recv2, based))
    rest = run_add_own(core, flags[1], rest, recv2)
    return run_add_late(core, out, rest, sib2).reshape(rows_dev, cols_dev)


def solution(mesh):
    fine = Mesh(mesh.devices.reshape(4, 2, 4, 2, 2), ALL)
    spec = P(("y", "zh"), ("x", "zl", "core"))
    return jax.shard_map(body, mesh=fine, in_specs=(spec, spec, P()), out_specs=spec, check_vma=False)
```

```python
import jax
import jax.numpy as jnp
from jax import lax
from jax.experimental import pallas as pl
from jax.experimental.pallas import tpu as pltpu
from jax.sharding import Mesh
from jax.sharding import PartitionSpec as P

CHIP = ("y", "zh", "x", "zl")
ALL = CHIP + ("core",)
CORE_SWAP = [(0, 1), (1, 0)]
VMEM = pl.BlockSpec(memory_space=pltpu.VMEM)
SMEM = pl.BlockSpec(memory_space=pltpu.SMEM)
HBM = pl.BlockSpec(memory_space=pltpu.HBM)
F32 = jnp.float32


def call(kernel, out_shape, in_specs, out_specs, name, moved, scratch=(), aliases=None, limit=16):
    many = isinstance(out_shape, tuple)
    outs = zip(out_shape, out_specs) if many else ((out_shape, out_specs),)
    outs = tuple(pltpu.HBM(array.shape, array.dtype) if spec is HBM else array for array, spec in outs)
    run = pl.pallas_call(
        kernel,
        out_shape=outs if many else outs[0],
        in_specs=in_specs,
        out_specs=out_specs,
        scratch_shapes=scratch,
        input_output_aliases=aliases or {},
        compiler_params=pltpu.CompilerParams(vmem_limit_bytes=limit << 20),
        cost_estimate=pl.CostEstimate(flops=0, bytes_accessed=moved, transcendentals=0),
        name=name,
    )

    def placed(*args):
        return run(*(
            pltpu.with_memory_space_constraint(arg, pltpu.HBM) if spec is HBM else arg
            for arg, spec in zip(args, in_specs)
        ))

    return placed


def shape(*dims):
    return jax.ShapeDtypeStruct(dims, F32)


TOKEN = shape(8, 128)


def run_lift(updates, front, bs):
    rows = updates.shape[0]
    half = bs // 2

    cuts = 4
    some = half // cuts

    def lift(updates, front, low, high, token, ucol, fcol, sems):
        def read(i, cut, core):
            whole, part = ((updates, ucol), (front, fcol))[i]
            here = pl.ds(core * half + cut * some, some)
            return pltpu.make_async_copy(
                whole.at[:, here, pl.ds(0, bs)], part.reshape(17, bs, bs).at[pl.ds(0, 16), here], sems.at[i, cut, core]
            )

        pieces = [(i, cut, core) for cut in range(cuts) for i in range(2) for core in range(2)]
        for piece in pieces:
            read(*piece).start()
        token[...] = jnp.zeros_like(token)
        for i, cut, core in pieces:
            read(i, cut, core).wait()
            part, out = (ucol, fcol)[i], (low, high)[core]

            def one(n, carry):
                chip = cut * some + n
                out[chip, 16 * i:16 * i + 16] = part[pl.ds(core * half + chip, 16, stride=bs), :]
                return carry

            lax.fori_loop(0, some, one, 0, unroll=8)

    share = shape(half, 32, bs)
    blocks = (16, bs, updates.shape[1])
    return call(
        lift, (share, share, TOKEN), [HBM, HBM], (VMEM,) * 3, "lift", 16 * rows * bs,
        [pltpu.VMEM((rows + bs, bs), F32)] * 2 + [pltpu.SemaphoreType.DMA((2, cuts, 2))],
    )(updates.reshape(blocks), front.reshape(blocks))


def run_pack(blocks, wait, gi, at, rows, extra, child_map=None):
    bs = blocks.shape[1]
    more = child_map is not None

    def pack(blocks, wait, *rest):
        out = rest[1] if more else rest[0]
        held, parted, read_sems, write_sems = rest[-4:]

        def read(j):
            return pltpu.make_async_copy(blocks.at[8 * gi + j, pl.ds(at, rows)], held.at[j], read_sems.at[j])

        def write(j):
            some = pl.ds(8 * j, 8)
            return pltpu.make_async_copy(parted.at[some], out.at[some, pl.ds(0, rows)], write_sems.at[j])

        for j in range(8):
            read(j).start()
        if more:
            whole_map, _, ends, adds, entries, sems = rest[:6]
            last = pltpu.make_async_copy(blocks.at[pl.ds(0, 8), pl.ds(bs - 8, 8)], ends, sems.at[0])
            fetch = pltpu.make_async_copy(whole_map, entries, sems.at[1])
            last.start()
            fetch.start()
        for j in range(8):
            read(j).wait()
            for jc in range(8):
                parted[8 * j + jc] = held[j, :, jc * bs:(jc + 1) * bs]
            write(j).start()
        if more:
            y, zh, x, zl, _ = (lax.axis_index(a) for a in ALL)
            me, col_pair = 2 * y + zh, 2 * x + zl
            last.wait()
            fetch.wait()
            live = (col_pair == 0) & (entries[me // 4, 0] // 8 % 2 == 0)
            place = lax.broadcasted_iota(jnp.int32, (16, bs), 0)
            for g in range(2):
                group = 2 * (me % 4) + g
                to = jnp.where(live, 8 * (entries[me // 4, 8 * group + me] // 8 % 2) + group, -1)
                adds[g] = jnp.where(place == to, 1.0, 0.0)
        for j in range(8):
            write(j).wait()

    load = shape(64, rows + extra, bs)
    scratch = [
        pltpu.VMEM((8, rows, 8 * bs), F32), pltpu.VMEM((64, rows, bs), F32), pltpu.SemaphoreType.DMA((8,)),
        pltpu.SemaphoreType.DMA((8,)),
    ]
    if not more:
        return call(pack, load, [HBM, VMEM], HBM, "pack", 512 * rows * bs, scratch)(blocks, wait)
    return call(
        pack, (load, shape(8, 8, 8 * bs), shape(2, 16, bs)), [HBM, VMEM, HBM], (HBM, VMEM, VMEM), "pack", 512 * rows * bs,
        [pltpu.SMEM(child_map.shape, jnp.int32), pltpu.SemaphoreType.DMA((2,))] + scratch,
    )(blocks, wait, child_map)


def run_put_rows(adds, ends, load, low, other, rows):
    bs = low.shape[-1]

    def put_rows(adds, ends, load, low, other, out, token, region, sems):
        y, zh, x, zl, t = (lax.axis_index(a) for a in ALL)
        me, col_pair = 2 * y + zh, 2 * x + zl
        token[...] = jnp.zeros_like(token)
        for c, part in ((0, low), (1, other)):
            @pl.when(t == c)
            def _():
                region[...] = part[...]

        @pl.when(col_pair == 0)
        def _():
            for at in range(64):
                own = [region[at, pl.ds(8 * g + me, 1), :] for g in range(2)]
                region[at, 16:32] += adds[0] * own[0] + adds[1] * own[1]

        slot = pl.ds(jnp.where(col_pair == 4, slot_of(0, 4), slot_of(me, 0)), 1)
        copies = []
        for j in range(8):
            for jc in range(8):
                region[8 * j + jc, slot, :] = ends[j, 7:8, jc * bs:(jc + 1) * bs]
            some = pl.ds(8 * j, 8)
            copies.append(pltpu.make_async_copy(region.at[some], out.at[some, pl.ds(rows, 32)], sems.at[j]))
            copies[-1].start()
        for copy in copies:
            copy.wait()

    return call(
        put_rows, (shape(*load.shape), TOKEN), [VMEM, VMEM, HBM, VMEM, VMEM], (HBM, VMEM), "put_rows", 8 * other.size,
        [pltpu.VMEM(low.shape, F32), pltpu.SemaphoreType.DMA((8,))], aliases={2: 0},
    )(adds, ends, load, low, other)


def run_sum_rows(marks, recv, ends, load, first):
    bs = recv.shape[-1]
    last = load.shape[1] - 40

    def sum_rows(marks, recv, ends, load, out, token, kids, total, rows, sems):
        token[...] = jnp.zeros_like(token)
        for up in range(2):
            for sr in range(4):
                acc = jnp.zeros((16, bs), F32)
                for h in range(2):
                    for v in range(2):
                        acc += marks[up, sr, 2 * v + h] * recv[(4 * h + sr) * 8 + 4 * v, first:first + 16]
                kids[pl.ds((up * 4 + sr) * 16, 16)] = acc
        for j in range(8):
            total[j] = kids[pl.ds(j, 16, stride=8), :] + recv[8 * j, first + 16:first + 32]
        copies = []
        for j in range(8):
            for jc in range(8):
                at = 8 * j + jc
                rows[at, 0:8] = ends[j, :, jc * bs:(jc + 1) * bs]
                rows[at, 7:8] = total[0, 0:1]
                rows[at, 8:24] = total[j]
                rows[at, 24:40] = total[jc]
            some = pl.ds(8 * j, 8)
            copies.append(pltpu.make_async_copy(rows.at[some], out.at[some, pl.ds(last, 40)], sems.at[j]))
            copies[-1].start()
        for copy in copies:
            copy.wait()

    return call(
        sum_rows, (shape(*load.shape), TOKEN), [VMEM, VMEM, VMEM, HBM], (HBM, VMEM), "sum_rows", 64 * 40 * bs * 8,
        [
            pltpu.VMEM((136, bs), F32), pltpu.VMEM((8, 16, bs), F32), pltpu.VMEM((64, 40, bs), F32),
            pltpu.SemaphoreType.DMA((8,)),
        ],
        aliases={3: 0},
    )(marks, recv, ends, load)


def add_blocks(flags, recv, sr, scp, here, sides, behind=None):
    sums = {}
    for h in range(2):
        for v in range(2):
            source, col_pair = 4 * h + sr, 4 * v + scp
            rows = here if behind is None else pl.ds(behind + slot_of(source, col_pair), 1)
            block = recv[source * 8 + col_pair, rows]
            for up in range(2):
                for side in sides:
                    term = flags[((((h + 2 * v) * 4 + sr) * 4 + scp) * 2 + up) * 2 + side] * block
                    sums[up, side] = sums[up, side] + term if (up, side) in sums else term
    return sums


def slot_of(row, col_pair):
    return 16 if col_pair == 4 else 8 + row


def child_sums(flags, recv, outs, held, sems, rows):
    step = 32
    more = held[0].shape[3] > rows

    def write(side, sr):
        return pltpu.make_async_copy(held[side].at[:, sr], outs[side].at[:, sr], sems.at[side, sr])

    for sr in range(4):
        def one(i, carry):
            at = pl.multiple_of(i * step, step)
            for scp in range(4):
                sums = add_blocks(flags, recv, sr, scp, pl.ds(at, step), (0, 1))
                for up in range(2):
                    for side in range(2):
                        held[side][up, sr, scp, pl.ds(at, step)] = sums[up, side]
            return carry

        lax.fori_loop(0, rows // step, one, 0)
        for scp in range(4) if more else ():
            sums = add_blocks(flags, recv, sr, scp, None, (0, 1), rows)
            for up in range(2):
                for side in range(2):
                    held[side][up, sr, scp, rows:rows + 1] = sums[up, side]
        for side in range(2):
            write(side, sr).start()

    def finish():
        for sr in range(4):
            for side in range(2):
                write(side, sr).wait()

    return finish


def sums_scratch(rows, bs):
    return [pltpu.VMEM((2, 4, 4, rows, bs), F32)] * 2 + [pltpu.SemaphoreType.DMA((2, 4))]


def run_child_sums(flags, recv, wait, rows, bs):
    def kernel(flags, recv, wait, own, sib, token, *held):
        token[...] = jnp.zeros_like(token)
        child_sums(flags, recv, (own, sib), held[:2], held[2], rows)()

    part = shape(2, 4, 4, rows + 8, bs)
    return call(
        kernel, (part, part, TOKEN), [SMEM, VMEM, VMEM], (HBM, HBM, VMEM), "child_sums", 64 * rows * bs * 8,
        sums_scratch(rows + 8, bs),
    )(flags, recv, wait)


def run_assemble(core, flags, mine, other, first):
    chips, width, bs = mine.shape
    half = bs // 2

    wide = width - first + 8

    def assemble(core, flags, mine, other, slabs, corner, own, sib, here, there, out, sems, *held):
        t = core[0]
        copies = [
            pltpu.make_async_copy(
                mine.at[:, pl.ds(first - 8, wide)], here.reshape(chips + 1, wide, bs).at[pl.ds(0, chips)], sems.at[0]
            ),
            pltpu.make_async_copy(other, there.reshape(chips + 1, wide, bs).at[pl.ds(0, chips)], sems.at[1]),
        ]
        for copy in copies:
            copy.start()
        finish = child_sums(flags, mine, (own, sib), held[:2], held[2], first)
        for who, (copy, part) in enumerate(zip(copies, (here, there))):
            copy.wait()
            rows_at = pl.multiple_of(half * (t if who == 0 else 1 - t), half)
            for s in range(25):
                start = 8 + s if s < 16 else 8 + s + 8 * t if s < 24 else 7
                rows = part[pl.ds(start, half, stride=wide), :]
                if s < 24:
                    out[s, pl.ds(rows_at, half)] = rows
                else:
                    corner[pl.ds(rows_at, half)] = rows
        copy = pltpu.make_async_copy(out, slabs, sems.at[2])
        copy.start()
        finish()
        copy.wait()

    part = shape(2, 4, 4, first, bs)
    return call(
        assemble, (shape(24, bs, bs), shape(bs, bs), part, part), [SMEM, SMEM, VMEM, HBM], (HBM, VMEM, HBM, HBM),
        "assemble", 200 * bs * bs,
        [pltpu.VMEM(((chips + 1) * wide, bs), F32)] * 2 + [pltpu.VMEM((24, bs, bs), F32), pltpu.SemaphoreType.DMA((3,))]
        + sums_scratch(first, bs),
    )(core, flags, mine, other)


def split(a):
    high = a.astype(jnp.bfloat16)
    left = a - high.astype(F32)
    mid = left.astype(jnp.bfloat16)
    return high, mid, (left - mid.astype(F32)).astype(jnp.bfloat16)


def spread(left, mine, other):
    return jnp.where(left, mine, other), jnp.where(left, other, mine)


def pair(scp, bs):
    return slice(2 * scp * bs, (2 * scp + 1) * bs), slice((2 * scp + 1) * bs, (2 * scp + 2) * bs)


def run_base(edge, front, solved, head, early, bs):
    rows, cols = front.shape
    blocks, tile, step = rows // bs, 256, 32
    cut = early[0].shape[3] - 8

    group = 4

    def base(edge, front, solved, head, own0, sib0, own1, sib1, out, rest, token, held, right, o0, s0, o1, s1, sems, more, back):
        top, col_zero, left = edge[0] == 1, edge[1] == 1, edge[2] == 0
        token[...] = jnp.zeros_like(token)

        def read(i):
            return pltpu.make_async_copy(front.at[i], held.at[i], sems.at[i])

        def write(i, to):
            return pltpu.make_async_copy(held.at[i], to.at[i // 2, pl.ds(0, bs)], back.at[i])

        sums = [
            pltpu.make_async_copy(src, dst, more.at[n])
            for n, (src, dst) in enumerate(((own0, o0), (sib0, s0), (own1, o1), (sib1, s1)))
        ]
        for i in range(blocks):
            read(i).start()
            if i == group - 1:
                for copy in sums:
                    copy.start()

        for at in range(0, cols, bs):
            high, mid, low = split(solved[rows + at:rows + at + bs])
            right[at:at + bs] = jnp.concatenate([high, high, mid, high, mid, low], axis=1)

        def some(q, carry):
            own = solved[pl.ds(pl.multiple_of(q * group * bs, group * bs), group * bs)]
            high, mid, low = split(own)
            parts = jnp.concatenate([high, mid, high, low, mid, high], axis=1)
            for n in range(group):
                read(q * group + n).wait()
            for at in range(0, cols, tile):
                lanes = slice(at, at + tile)
                product = lax.dot_general(
                    parts, right[at:at + tile], (((1,), (1,)), ((), ())), preferred_element_type=F32
                )
                for n in range(group):
                    keep = jnp.where(top & (q == 0), 0.0, 1.0) if n == 0 else 1.0
                    held[q * group + n, :, lanes] -= keep * product[n * bs:(n + 1) * bs]

            @pl.when(col_zero)
            def _():
                for n in range(group):
                    held[q * group + n, :, 0:bs] = own[n * bs:(n + 1) * bs]

            @pl.when(top & col_zero & (q == 0))
            def _():
                held[0, :, 0:bs] = head[...]

            @pl.when(q == 0)
            def _():
                for copy in sums:
                    copy.wait()
                for late, soon in ((o1, o0), (s1, s0)):
                    late[:, :, :, bs - cut - 1:bs - cut] = soon[:, :, :, cut:cut + 1]

            for n in range(0, group, 2):
                i = q * group + n
                up, sr = i // 8, i // 2 % 4
                for at in range(0, bs, step):
                    here = slice(at, at + step)
                    own, sib, inner = (o0, s0, at) if at < cut else (o1, s1, at - cut)
                    for scp in range(4):
                        two = spread(left, own[up, sr, scp, inner:inner + step], sib[up, sr, scp, inner:inner + step])
                        for lanes, add in zip(pair(scp, bs), two):
                            held[i, here, lanes] += add
                write(i, out).start()
                write(i + 1, rest).start()
            return carry

        lax.fori_loop(0, blocks // group, some, 0)

        def finish(n, carry):
            write(2 * n, out).wait()
            write(2 * n + 1, rest).wait()
            return carry

        lax.fori_loop(0, blocks // 2, finish, 0)

    parts = [pltpu.VMEM(a.shape, F32) for a in early]
    return call(
        base, (shape(blocks // 2, 2 * bs, cols), shape(blocks // 2, bs, cols), TOKEN), [SMEM, HBM, VMEM, VMEM] + [HBM] * 4,
        (HBM, HBM, VMEM), "base", rows * cols * 8,
        [pltpu.VMEM((blocks, bs, cols), F32), pltpu.VMEM((cols, 6 * bs), jnp.bfloat16)] + parts
        + [pltpu.SemaphoreType.DMA((n,)) for n in (blocks, 4, blocks)],
        limit=28,
    )(edge, front.reshape(blocks, bs, cols), solved, head, *early)


def run_late_sums(flags, recv, wait):
    chips, bs, _ = recv.shape
    step = 32

    def late_sums(all_flags, recv, wait, sib, flags, held, flag_sem, sems):
        fetch = pltpu.make_async_copy(all_flags, flags, flag_sem)
        fetch.start()

        def read(sr, h):
            some = pl.ds((4 * h + sr) * 8, 8)
            return pltpu.make_async_copy(recv.at[some], held.at[some], sems.at[2 * sr + h])

        for sr in range(4):
            for h in range(2):
                read(sr, h).start()
        fetch.wait()
        for sr in range(4):
            for h in range(2):
                read(sr, h).wait()

            def one(i, carry):
                here = pl.ds(pl.multiple_of(i * step, step), step)
                for scp in range(4):
                    sums = add_blocks(flags, held, sr, scp, here, (1,))
                    for up in range(2):
                        sib[up, sr, scp, here] = sums[up, 1]
                return carry

            lax.fori_loop(0, bs // step, one, 0)

    return call(
        late_sums, shape(2, 4, 4, bs, bs), [HBM, HBM, VMEM], VMEM, "late_sums", 96 * bs * bs * 4,
        [
            pltpu.SMEM(flags.shape, F32), pltpu.VMEM((chips, bs, bs), F32), pltpu.SemaphoreType.DMA,
            pltpu.SemaphoreType.DMA((8,)),
        ],
    )(flags, recv, wait)


def run_add_own(flags, rest, recv):
    blocks, bs, cols = rest.shape
    step = 32

    def add_own(all_flags, rest, recv, out, flags, held, flag_sem, sems, more):
        fetch = pltpu.make_async_copy(all_flags, flags, flag_sem)
        fetch.start()
        left = lax.axis_index("core") == 0

        def read(sr, h):
            some = pl.ds((4 * h + sr) * 8, 8)
            return pltpu.make_async_copy(recv.at[some], held.at[some], sems.at[2 * sr + h])

        def base(i):
            return pltpu.make_async_copy(rest.at[i], out.at[i], more.at[i])

        for sr in range(4):
            for n in range(2):
                read(sr, n).start()
                base(4 * n + sr).start()
        fetch.wait()
        for sr in range(4):
            for n in range(2):
                read(sr, n).wait()
                base(4 * n + sr).wait()

            def one(i, carry):
                here = pl.ds(pl.multiple_of(i * step, step), step)
                for scp in range(4):
                    sums = add_blocks(flags, held, sr, scp, here, (0,))
                    for up in range(2):
                        two = spread(left, sums[up, 0], 0.0)
                        for lanes, add in zip(pair(scp, bs), two):
                            out[4 * up + sr, here, lanes] += add
                return carry

            lax.fori_loop(0, bs // step, one, 0)

    return call(
        add_own, shape(blocks, bs, cols), [HBM, HBM, HBM], VMEM, "add_own", blocks * bs * cols * 12,
        [
            pltpu.SMEM(flags.shape, F32), pltpu.VMEM(recv.shape, F32), pltpu.SemaphoreType.DMA,
            pltpu.SemaphoreType.DMA((8,)), pltpu.SemaphoreType.DMA((8,)),
        ],
    )(flags, rest, recv)


def run_add_late(out, rest, sib):
    blocks, bs, cols = rest.shape
    step = 32

    def add_late(before, rest, sib, out, done, sems):
        left = lax.axis_index("core") == 0

        def write(i):
            return pltpu.make_async_copy(done.at[i], out.at[i, pl.ds(bs, bs)], sems.at[i])

        def one(i, carry):
            up, sr = i // 4, i % 4
            for at in range(0, bs, step):
                here = slice(at, at + step)
                for scp in range(4):
                    for lanes, add in zip(pair(scp, bs), spread(left, 0.0, sib[up, sr, scp, here])):
                        done[i, here, lanes] = rest[i, here, lanes] + add
            write(i).start()
            return carry

        lax.fori_loop(0, blocks, one, 0)
        lax.fori_loop(0, blocks, lambda i, c: (write(i).wait(), c)[1], 0)

    return call(
        add_late, shape(*out.shape), [HBM, VMEM, VMEM], HBM, "add_late", out.size * 6,
        [pltpu.VMEM((blocks, bs, cols), F32), pltpu.SemaphoreType.DMA((blocks,))], aliases={0: 0},
    )(out, rest, sib)


def body(front, updates, child_map):
    rows_dev, cols_dev = front.shape
    bs = rows_dev // 16
    half = bs // 2
    y, zh, x, zl, t = (lax.axis_index(a) for a in ALL)
    ji, jc = 2 * y + zh, 2 * x + zl
    col = 2 * jc + t
    core = t.reshape(1).astype(jnp.int32)
    blocks = updates.reshape(16, bs, cols_dev)

    def swap(a):
        return lax.ppermute(a, "core", CORE_SWAP)

    def send(load):
        return lax.all_to_all(load, CHIP, 0, 0, tiled=True)

    bits = (child_map.reshape(4, 8, 8) // 8) % 2
    col_bits = lax.dynamic_index_in_dim(bits, jc, 2, keepdims=False).reshape(4, 4, 2)
    col_bits = lax.dynamic_index_in_dim(col_bits, t, 2, keepdims=False)
    row_bits = lax.dynamic_index_in_dim(bits, ji, 2, keepdims=False).reshape(4, 4, 2)
    in_panel = (col == 0) & (jnp.arange(4) == 0)
    side = jnp.stack([(col_bits == t) & ~in_panel, col_bits != t], -1)
    up = row_bits[..., None] == jnp.arange(2)
    flags = [
        (up[:, :, gi, None, :, None] & side[:, None, :, None, :]).astype(F32).reshape(-1) for gi in range(2)
    ]
    live = bits[:, 0, 0] == 0
    marks = (bits.reshape(4, 4, 16).transpose(1, 0, 2) == jnp.arange(2)[:, None, None, None]) & live[:, None]
    sr_at, h_at, j_at = jnp.arange(4)[:, None, None], jnp.arange(4)[None, :, None], jnp.arange(16)[None, None] % 8
    marks &= ~((h_at < 2) & (4 * h_at + sr_at == j_at))
    marks = jnp.broadcast_to(marks.astype(F32)[..., None], (2, 4, 4, 16, bs))

    low, high, lifted = run_lift(updates, front, bs)
    other = lax.ppermute(high, ALL, [((r * 8 + q) * 2, (r * 8 + q) * 2 + 1) for r in range(8) for q in (0, 4)])
    load0, ends, adds = run_pack(blocks, lifted, 0, 0, half, 32, child_map)
    load0, sent0 = run_put_rows(adds, ends, load0, low, other, half)
    recv0 = send(load0)

    load1, sent1 = run_sum_rows(marks, recv0, ends, run_pack(blocks, sent0, 0, half, half, 32), half)
    recv1 = send(load1)
    own0, sib0, summed0 = run_child_sums(flags[0], recv0, sent1, half, bs)
    sib0 = swap(sib0)

    recv2 = send(run_pack(blocks, summed0, 1, 0, bs, 0))

    slabs, corner, own1, sib1 = run_assemble(core, flags[0], recv1, swap(recv1[:, half - 8:]), half)
    sib1 = swap(sib1)
    head = jnp.linalg.cholesky(corner)
    solved = lax.linalg.triangular_solve(
        head, slabs.reshape(24 * bs, bs), left_side=False, lower=True, transpose_a=True
    )
    edge = jnp.stack([ji == 0, col == 0, t == 1]).astype(jnp.int32)
    out, rest, based = run_base(edge, front, solved, head, (own0, sib0, own1, sib1), bs)

    sib2 = swap(run_late_sums(flags[1], recv2, based))
    rest = run_add_own(flags[1], rest, recv2)
    return run_add_late(out, rest, sib2).reshape(rows_dev, cols_dev)


def solution(mesh):
    fine = Mesh(mesh.devices.reshape(4, 2, 4, 2, 2), ALL)
    spec = P(("y", "zh"), ("x", "zl", "core"))
    return jax.shard_map(body, mesh=fine, in_specs=(spec, spec, P()), out_specs=spec, check_vma=False)
```

```python
import jax
import jax.numpy as jnp
from jax import lax
from jax.experimental import pallas as pl
from jax.experimental.pallas import tpu as pltpu
from jax.sharding import Mesh
from jax.sharding import PartitionSpec as P

CHIP = ("y", "zh", "x", "zl")
ALL = CHIP + ("core",)
CORE_SWAP = [(0, 1), (1, 0)]
VMEM = pl.BlockSpec(memory_space=pltpu.VMEM)
SMEM = pl.BlockSpec(memory_space=pltpu.SMEM)
HBM = pl.BlockSpec(memory_space=pltpu.HBM)
ANY = pl.BlockSpec(memory_space=pl.ANY)
F32 = jnp.float32


def call(kernel, out_shape, in_specs, out_specs, name, moved, scratch=(), aliases=None, limit=16):
    many = isinstance(out_shape, tuple)
    outs = zip(out_shape, out_specs) if many else ((out_shape, out_specs),)
    outs = tuple(pltpu.HBM(array.shape, array.dtype) if spec is HBM else array for array, spec in outs)
    run = pl.pallas_call(
        kernel,
        out_shape=outs if many else outs[0],
        in_specs=in_specs,
        out_specs=out_specs,
        scratch_shapes=scratch,
        input_output_aliases=aliases or {},
        compiler_params=pltpu.CompilerParams(vmem_limit_bytes=limit << 20),
        cost_estimate=pl.CostEstimate(flops=0, bytes_accessed=moved, transcendentals=0),
        name=name,
    )

    def placed(*args):
        return run(*(
            pltpu.with_memory_space_constraint(arg, pltpu.HBM) if spec is HBM else arg
            for arg, spec in zip(args, in_specs)
        ))

    return placed


def shape(*dims):
    return jax.ShapeDtypeStruct(dims, F32)


TOKEN = shape(8, 128)


def run_lift(updates, front, bs):
    rows = updates.shape[0]
    half = bs // 2

    cuts = 4
    some = half // cuts

    def lift(updates, front, low, high, token, ucol, fcol, sems):
        def read(i, cut, core):
            whole, part = ((updates, ucol), (front, fcol))[i]
            here = pl.ds(core * half + cut * some, some)
            return pltpu.make_async_copy(
                whole.at[:, here, pl.ds(0, bs)], part.reshape(17, bs, bs).at[pl.ds(0, 16), here], sems.at[i, cut, core]
            )

        pieces = [(i, cut, core) for cut in range(cuts) for i in range(2) for core in range(2)]
        for piece in pieces:
            read(*piece).start()
        token[...] = jnp.zeros_like(token)
        for i, cut, core in pieces:
            read(i, cut, core).wait()
            part, out = (ucol, fcol)[i], (low, high)[core]

            def one(n, carry):
                chip = cut * some + n
                out[chip, 16 * i:16 * i + 16] = part[pl.ds(core * half + chip, 16, stride=bs), :]
                return carry

            lax.fori_loop(0, some, one, 0, unroll=8)

    share = shape(half, 32, bs)
    blocks = (16, bs, updates.shape[1])
    return call(
        lift, (share, share, TOKEN), [HBM, HBM], (VMEM,) * 3, "lift", 16 * rows * bs,
        [pltpu.VMEM((rows + bs, bs), F32)] * 2 + [pltpu.SemaphoreType.DMA((2, cuts, 2))],
    )(updates.reshape(blocks), front.reshape(blocks))


def run_pack(blocks, wait, gi, at, rows, extra, child_map=None):
    bs = blocks.shape[1]
    more = child_map is not None

    def pack(blocks, wait, *rest):
        out = rest[1] if more else rest[0]
        held, parted, read_sems, write_sems = rest[-4:]

        def read(j):
            return pltpu.make_async_copy(blocks.at[8 * gi + j, pl.ds(at, rows)], held.at[j], read_sems.at[j])

        def write(j):
            some = pl.ds(8 * j, 8)
            return pltpu.make_async_copy(parted.at[some], out.at[some, pl.ds(0, rows)], write_sems.at[j])

        for j in range(8):
            read(j).start()
        if more:
            whole_map, _, ends, adds, entries, sems = rest[:6]
            last = pltpu.make_async_copy(blocks.at[pl.ds(0, 8), pl.ds(bs - 8, 8)], ends, sems.at[0])
            fetch = pltpu.make_async_copy(whole_map, entries, sems.at[1])
            last.start()
            fetch.start()
        for j in range(8):
            read(j).wait()
            for jc in range(8):
                parted[8 * j + jc] = held[j, :, jc * bs:(jc + 1) * bs]
            write(j).start()
        if more:
            y, zh, x, zl, _ = (lax.axis_index(a) for a in ALL)
            me, col_pair = 2 * y + zh, 2 * x + zl
            last.wait()
            fetch.wait()
            live = (col_pair == 0) & (entries[me // 4, 0] // 8 % 2 == 0)
            place = lax.broadcasted_iota(jnp.int32, (16, bs), 0)
            for g in range(2):
                group = 2 * (me % 4) + g
                to = jnp.where(live, 8 * (entries[me // 4, 8 * group + me] // 8 % 2) + group, -1)
                adds[g] = jnp.where(place == to, 1.0, 0.0)
        for j in range(8):
            write(j).wait()

    load = shape(64, rows + extra, bs)
    scratch = [
        pltpu.VMEM((8, rows, 8 * bs), F32), pltpu.VMEM((64, rows, bs), F32), pltpu.SemaphoreType.DMA((8,)),
        pltpu.SemaphoreType.DMA((8,)),
    ]
    if not more:
        return call(pack, load, [HBM, VMEM], HBM, "pack", 512 * rows * bs, scratch)(blocks, wait)
    return call(
        pack, (load, shape(8, 8, 8 * bs), shape(2, 16, bs)), [HBM, VMEM, HBM], (HBM, VMEM, VMEM), "pack", 512 * rows * bs,
        [pltpu.SMEM(child_map.shape, jnp.int32), pltpu.SemaphoreType.DMA((2,))] + scratch,
    )(blocks, wait, child_map)


def run_put_rows(adds, ends, load, low, other, rows):
    bs = low.shape[-1]

    def put_rows(adds, ends, load, low, other, out, token, region, sems):
        y, zh, x, zl, t = (lax.axis_index(a) for a in ALL)
        me, col_pair = 2 * y + zh, 2 * x + zl
        token[...] = jnp.zeros_like(token)
        slot = pl.ds(jnp.where(col_pair == 4, slot_of(0, 4), slot_of(me, 0)), 1)
        copies = []
        for j in range(8):
            some = slice(8 * j, 8 * j + 8)
            region[some] = jnp.where(t == 0, low[some], other[some])
            for jc in range(8):
                at = 8 * j + jc
                own = [region[at, pl.ds(8 * g + me, 1), :] for g in range(2)]
                region[at, 16:32] += adds[0] * own[0] + adds[1] * own[1]
                region[at, slot, :] = ends[j, 7:8, jc * bs:(jc + 1) * bs]
            some = pl.ds(8 * j, 8)
            copies.append(pltpu.make_async_copy(region.at[some], out.at[some, pl.ds(rows, 32)], sems.at[j]))
            copies[-1].start()
        for copy in copies:
            copy.wait()

    return call(
        put_rows, (shape(*load.shape), TOKEN), [VMEM, VMEM, HBM, VMEM, VMEM], (HBM, VMEM), "put_rows", 8 * other.size,
        [pltpu.VMEM(low.shape, F32), pltpu.SemaphoreType.DMA((8,))], aliases={2: 0},
    )(adds, ends, load, low, other)


def run_sum_rows(marks, recv, ends, load, first):
    bs = recv.shape[-1]
    last = load.shape[1] - 40

    def sum_rows(marks, recv, ends, load, out, token, kids, total, rows, sems):
        token[...] = jnp.zeros_like(token)
        for up in range(2):
            for sr in range(4):
                acc = jnp.zeros((16, bs), F32)
                for h in range(2):
                    for v in range(2):
                        acc += marks[up, sr, 2 * v + h] * recv[(4 * h + sr) * 8 + 4 * v, first:first + 16]
                kids[pl.ds((up * 4 + sr) * 16, 16)] = acc
        for j in range(8):
            total[j] = kids[pl.ds(j, 16, stride=8), :] + recv[8 * j, first + 16:first + 32]
        copies = []
        for j in range(8):
            for jc in range(8):
                at = 8 * j + jc
                rows[at, 0:8] = ends[j, :, jc * bs:(jc + 1) * bs]
                rows[at, 7:8] = total[0, 0:1]
                rows[at, 8:24] = total[j]
                rows[at, 24:40] = total[jc]
            some = pl.ds(8 * j, 8)
            copies.append(pltpu.make_async_copy(rows.at[some], out.at[some, pl.ds(last, 40)], sems.at[j]))
            copies[-1].start()
        for copy in copies:
            copy.wait()

    return call(
        sum_rows, (shape(*load.shape), TOKEN), [VMEM, VMEM, VMEM, HBM], (HBM, VMEM), "sum_rows", 64 * 40 * bs * 8,
        [
            pltpu.VMEM((136, bs), F32), pltpu.VMEM((8, 16, bs), F32), pltpu.VMEM((64, 40, bs), F32),
            pltpu.SemaphoreType.DMA((8,)),
        ],
        aliases={3: 0},
    )(marks, recv, ends, load)


def add_blocks(flags, recv, sr, scp, here, sides, behind=None):
    sums = {}
    for h in range(2):
        for v in range(2):
            source, col_pair = 4 * h + sr, 4 * v + scp
            rows = here if behind is None else pl.ds(behind + slot_of(source, col_pair), 1)
            block = recv[source * 8 + col_pair, rows]
            for up in range(2):
                for side in sides:
                    term = flags[((((h + 2 * v) * 4 + sr) * 4 + scp) * 2 + up) * 2 + side] * block
                    sums[up, side] = sums[up, side] + term if (up, side) in sums else term
    return sums


def slot_of(row, col_pair):
    return 16 if col_pair == 4 else 8 + row


def child_sums(flags, recv, outs, held, sems, rows):
    step = 32
    more = held[0].shape[3] > rows

    def write(side, sr):
        return pltpu.make_async_copy(held[side].at[:, sr], outs[side].at[:, sr], sems.at[side, sr])

    for sr in range(4):
        def one(i, carry):
            at = pl.multiple_of(i * step, step)
            for scp in range(4):
                sums = add_blocks(flags, recv, sr, scp, pl.ds(at, step), (0, 1))
                for up in range(2):
                    for side in range(2):
                        held[side][up, sr, scp, pl.ds(at, step)] = sums[up, side]
            return carry

        lax.fori_loop(0, rows // step, one, 0)
        for scp in range(4) if more else ():
            sums = add_blocks(flags, recv, sr, scp, None, (0, 1), rows)
            for up in range(2):
                for side in range(2):
                    held[side][up, sr, scp, rows:rows + 1] = sums[up, side]
        for side in range(2):
            write(side, sr).start()

    def finish():
        for sr in range(4):
            for side in range(2):
                write(side, sr).wait()

    return finish


def sums_scratch(rows, bs):
    return [pltpu.VMEM((2, 4, 4, rows, bs), F32)] * 2 + [pltpu.SemaphoreType.DMA((2, 4))]


def run_child_sums(flags, recv, wait, rows, bs):
    def kernel(flags, recv, wait, own, sib, token, *held):
        token[...] = jnp.zeros_like(token)
        child_sums(flags, recv, (own, sib), held[:2], held[2], rows)()

    part = shape(2, 4, 4, rows + 8, bs)
    return call(
        kernel, (part, part, TOKEN), [SMEM, VMEM, VMEM], (HBM, HBM, VMEM), "child_sums", 64 * rows * bs * 8,
        sums_scratch(rows + 8, bs),
    )(flags, recv, wait)


def run_assemble(core, flags, mine, other, first):
    chips, width, bs = mine.shape
    half = bs // 2

    wide = width - first + 8

    def assemble(core, flags, mine, other, slabs, corner, own, sib, here, there, out, sems, *held):
        t = core[0]
        copies = [
            pltpu.make_async_copy(
                mine.at[:, pl.ds(first - 8, wide)], here.reshape(chips + 1, wide, bs).at[pl.ds(0, chips)], sems.at[0]
            ),
            pltpu.make_async_copy(other, there.reshape(chips + 1, wide, bs).at[pl.ds(0, chips)], sems.at[1]),
        ]
        for copy in copies:
            copy.start()
        finish = child_sums(flags, mine, (own, sib), held[:2], held[2], first)
        for who, (copy, part) in enumerate(zip(copies, (here, there))):
            copy.wait()
            rows_at = pl.multiple_of(half * (t if who == 0 else 1 - t), half)
            for s in range(25):
                start = 8 + s if s < 16 else 8 + s + 8 * t if s < 24 else 7
                rows = part[pl.ds(start, half, stride=wide), :]
                if s < 24:
                    out[s, pl.ds(rows_at, half)] = rows
                else:
                    corner[pl.ds(rows_at, half)] = rows
        copy = pltpu.make_async_copy(out, slabs, sems.at[2])
        copy.start()
        finish()
        copy.wait()

    part = shape(2, 4, 4, first, bs)
    return call(
        assemble, (shape(24, bs, bs), shape(bs, bs), part, part), [SMEM, SMEM, VMEM, ANY], (HBM, VMEM, HBM, HBM),
        "assemble", 200 * bs * bs,
        [pltpu.VMEM(((chips + 1) * wide, bs), F32)] * 2 + [pltpu.VMEM((24, bs, bs), F32), pltpu.SemaphoreType.DMA((3,))]
        + sums_scratch(first, bs),
    )(core, flags, mine, other)


def split(a):
    high = a.astype(jnp.bfloat16)
    left = a - high.astype(F32)
    mid = left.astype(jnp.bfloat16)
    return high, mid, (left - mid.astype(F32)).astype(jnp.bfloat16)


def spread(left, mine, other):
    return jnp.where(left, mine, other), jnp.where(left, other, mine)


def pair(scp, bs):
    return slice(2 * scp * bs, (2 * scp + 1) * bs), slice((2 * scp + 1) * bs, (2 * scp + 2) * bs)


def run_base(edge, front, solved, head, early, bs):
    rows, cols = front.shape
    blocks, tile, step = rows // bs, 256, 32
    cut = early[0].shape[3] - 8

    group = 4

    def base(edge, front, solved, head, own0, sib0, own1, sib1, out, rest, token, held, right, o0, s0, o1, s1, sems, more, back, parts_back):
        top, col_zero, left = edge[0] == 1, edge[1] == 1, edge[2] == 0
        token[...] = jnp.zeros_like(token)

        def read(i):
            return pltpu.make_async_copy(front.at[i], held.at[i], sems.at[i])

        def write(n):
            return pltpu.make_async_copy(held.at[2 * n], out.at[n, pl.ds(0, bs)], back.at[n])

        def part(n, c):
            return pltpu.make_async_copy(held.at[2 * n + 1, :, pl.ds(c * bs, bs)], rest.at[c, n], parts_back.at[c, n])

        sums = [
            pltpu.make_async_copy(src, dst, more.at[n])
            for n, (src, dst) in enumerate(((own0, o0), (sib0, s0), (own1, o1), (sib1, s1)))
        ]
        for i in range(blocks):
            read(i).start()
            if i == group - 1:
                for copy in sums:
                    copy.start()

        for at in range(0, cols, bs):
            high, mid, low = split(solved[rows + at:rows + at + bs])
            right[at:at + bs] = jnp.concatenate([high, high, mid, high, mid, low], axis=1)

        def some(q, carry):
            own = solved[pl.ds(pl.multiple_of(q * group * bs, group * bs), group * bs)]
            high, mid, low = split(own)
            parts = jnp.concatenate([high, mid, high, low, mid, high], axis=1)
            for n in range(group):
                read(q * group + n).wait()
            for at in range(0, cols, tile):
                lanes = slice(at, at + tile)
                product = lax.dot_general(
                    parts, right[at:at + tile], (((1,), (1,)), ((), ())), preferred_element_type=F32
                )
                for n in range(group):
                    keep = jnp.where(top & (q == 0), 0.0, 1.0) if n == 0 else 1.0
                    held[q * group + n, :, lanes] -= keep * product[n * bs:(n + 1) * bs]

            @pl.when(col_zero)
            def _():
                for n in range(group):
                    held[q * group + n, :, 0:bs] = own[n * bs:(n + 1) * bs]

            @pl.when(top & col_zero & (q == 0))
            def _():
                held[0, :, 0:bs] = head[...]

            @pl.when(q == 0)
            def _():
                for copy in sums:
                    copy.wait()
                for late, soon in ((o1, o0), (s1, s0)):
                    late[:, :, :, bs - cut - 1:bs - cut] = soon[:, :, :, cut:cut + 1]

            for n in range(0, group, 2):
                i = q * group + n
                up, sr = i // 8, i // 2 % 4
                for at in range(0, bs, step):
                    here = slice(at, at + step)
                    own, sib, inner = (o0, s0, at) if at < cut else (o1, s1, at - cut)
                    for scp in range(4):
                        two = spread(left, own[up, sr, scp, inner:inner + step], sib[up, sr, scp, inner:inner + step])
                        for lanes, add in zip(pair(scp, bs), two):
                            held[i, here, lanes] += add
                write(i // 2).start()
                for c in range(cols // bs):
                    part(i // 2, c).start()
            return carry

        lax.fori_loop(0, blocks // group, some, 0)

        def finish(n, carry):
            write(n).wait()
            for c in range(cols // bs):
                part(n, c).wait()
            return carry

        lax.fori_loop(0, blocks // 2, finish, 0)

    parts = [pltpu.VMEM(a.shape, F32) for a in early]
    return call(
        base, (shape(blocks // 2, 2 * bs, cols), shape(cols // bs, blocks // 2, bs, bs), TOKEN), [SMEM, HBM, VMEM, VMEM] + [ANY] * 4,
        (HBM, HBM, VMEM), "base", rows * cols * 8,
        [pltpu.VMEM((blocks, bs, cols), F32), pltpu.VMEM((cols, 6 * bs), jnp.bfloat16)] + parts
        + [pltpu.SemaphoreType.DMA(n) for n in ((blocks,), (4,), (blocks // 2,), (cols // bs, blocks // 2))],
        limit=28,
    )(edge, front.reshape(blocks, bs, cols), solved, head, *early)


def run_late_sums(flags, recv, wait):
    chips, bs, _ = recv.shape
    step = 32

    def late_sums(all_flags, recv, wait, sib, held, flags, flag_sem, sems):
        fetch = pltpu.make_async_copy(all_flags, flags, flag_sem)
        fetch.start()

        def read(sr, h):
            some = pl.ds((4 * h + sr) * 8, 8)
            return pltpu.make_async_copy(recv.at[some], held.at[some], sems.at[2 * sr + h])

        for sr in range(4):
            for h in range(2):
                read(sr, h).start()
        fetch.wait()
        for sr in range(4):
            for h in range(2):
                read(sr, h).wait()

            def one(i, carry):
                here = pl.ds(pl.multiple_of(i * step, step), step)
                for scp in range(4):
                    sums = add_blocks(flags, held, sr, scp, here, (1,))
                    for up in range(2):
                        sib[up, sr, scp, here] = sums[up, 1]
                return carry

            lax.fori_loop(0, bs // step, one, 0)

    return call(
        late_sums, (shape(2, 4, 4, bs, bs), shape(*recv.shape)), [HBM, HBM, VMEM], (VMEM, VMEM), "late_sums", 96 * bs * bs * 4,
        [
            pltpu.SMEM(flags.shape, F32), pltpu.SemaphoreType.DMA,
            pltpu.SemaphoreType.DMA((8,)),
        ],
    )(flags, recv, wait)


def run_add_own(flags, out, rest, recv):
    bs, step = recv.shape[1], 32
    parts = rest.reshape(8, 2, 4, bs, bs)

    def add_own(all_flags, before, rest, held, out, others, flags, mine, flag_sem, own_sems, other_sems, back):
        fetch = pltpu.make_async_copy(all_flags, flags, flag_sem)
        fetch.start()
        t = lax.axis_index("core")

        def own(scp):
            return pltpu.make_async_copy(rest.at[2 * scp + t], mine.at[scp], own_sems.at[scp])

        def other(scp):
            return pltpu.make_async_copy(rest.at[2 * scp + 1 - t], others.at[scp], other_sems.at[scp])

        def write(sr, scp):
            lanes = pl.ds(pl.multiple_of((2 * scp + t) * bs, bs), bs)
            return pltpu.make_async_copy(mine.at[scp, :, sr], out.at[:, sr, pl.ds(bs, bs), lanes], back.at[sr, scp])

        for scp in range(4):
            own(scp).start()
        for scp in range(4):
            other(scp).start()
        fetch.wait()
        for scp in range(4):
            own(scp).wait()
        for sr in range(4):
            def one(i, carry):
                here = pl.ds(pl.multiple_of(i * step, step), step)
                for scp in range(4):
                    sums = add_blocks(flags, held, sr, scp, here, (0,))
                    for up in range(2):
                        mine[scp, up, sr, here] += sums[up, 0]
                return carry

            lax.fori_loop(0, bs // step, one, 0)
            for scp in range(4):
                write(sr, scp).start()
        for scp in range(4):
            other(scp).wait()
            for sr in range(4):
                write(sr, scp).wait()

    half = (4, 2, 4, bs, bs)
    return call(
        add_own, (shape(*out.shape), shape(*half)), [HBM] * 3 + [VMEM], (HBM, VMEM), "add_own", rest.size * 12,
        [pltpu.SMEM(flags.shape, F32), pltpu.VMEM(half, F32), pltpu.SemaphoreType.DMA]
        + [pltpu.SemaphoreType.DMA(n) for n in ((4,), (4,), (4, 4))],
        aliases={1: 0},
    )(flags, out, parts, recv)


def run_add_late(out, others, sib):
    bs, step = sib.shape[-1], 32

    def add_late(before, others, sib, out, done, sems):
        t = lax.axis_index("core")

        def write(scp, up):
            lanes = pl.ds(pl.multiple_of((2 * scp + 1 - t) * bs, bs), bs)
            return pltpu.make_async_copy(done.at[scp, up], out.at[up, :, pl.ds(bs, bs), lanes], sems.at[scp, up])

        for scp in range(4):
            for up in range(2):
                for sr in range(4):
                    for at in range(0, bs, step):
                        here = slice(at, at + step)
                        done[scp, up, sr, here] = others[scp, up, sr, here] + sib[up, sr, scp, here]
                write(scp, up).start()
        for scp in range(4):
            for up in range(2):
                write(scp, up).wait()

    return call(
        add_late, shape(*out.shape), [HBM, VMEM, VMEM], HBM, "add_late", others.size * 12,
        [pltpu.VMEM(others.shape, F32), pltpu.SemaphoreType.DMA((4, 2))], aliases={0: 0},
    )(out, others, sib)


def body(front, updates, child_map):
    rows_dev, cols_dev = front.shape
    bs = rows_dev // 16
    half = bs // 2
    y, zh, x, zl, t = (lax.axis_index(a) for a in ALL)
    ji, jc = 2 * y + zh, 2 * x + zl
    col = 2 * jc + t
    core = t.reshape(1).astype(jnp.int32)
    blocks = updates.reshape(16, bs, cols_dev)

    def swap(a):
        return lax.ppermute(a, "core", CORE_SWAP)

    def send(load):
        return lax.all_to_all(load, CHIP, 0, 0, tiled=True)

    bits = (child_map.reshape(4, 8, 8) // 8) % 2
    col_bits = lax.dynamic_index_in_dim(bits, jc, 2, keepdims=False).reshape(4, 4, 2)
    col_bits = lax.dynamic_index_in_dim(col_bits, t, 2, keepdims=False)
    row_bits = lax.dynamic_index_in_dim(bits, ji, 2, keepdims=False).reshape(4, 4, 2)
    in_panel = (col == 0) & (jnp.arange(4) == 0)
    side = jnp.stack([(col_bits == t) & ~in_panel, col_bits != t], -1)
    up = row_bits[..., None] == jnp.arange(2)
    flags = [
        (up[:, :, gi, None, :, None] & side[:, None, :, None, :]).astype(F32).reshape(-1) for gi in range(2)
    ]
    live = bits[:, 0, 0] == 0
    marks = (bits.reshape(4, 4, 16).transpose(1, 0, 2) == jnp.arange(2)[:, None, None, None]) & live[:, None]
    sr_at, h_at, j_at = jnp.arange(4)[:, None, None], jnp.arange(4)[None, :, None], jnp.arange(16)[None, None] % 8
    marks &= ~((h_at < 2) & (4 * h_at + sr_at == j_at))
    marks = jnp.broadcast_to(marks.astype(F32)[..., None], (2, 4, 4, 16, bs))

    low, high, lifted = run_lift(updates, front, bs)
    other = lax.ppermute(high, ALL, [((r * 8 + q) * 2, (r * 8 + q) * 2 + 1) for r in range(8) for q in (0, 4)])
    load0, ends, adds = run_pack(blocks, lifted, 0, 0, half, 32, child_map)
    load0, sent0 = run_put_rows(adds, ends, load0, low, other, half)
    recv0 = send(load0)

    load1, sent1 = run_sum_rows(marks, recv0, ends, run_pack(blocks, sent0, 0, half, half, 32), half)
    recv1 = send(load1)
    own0, sib0, summed0 = run_child_sums(flags[0], recv0, sent1, half, bs)
    sib0 = swap(sib0)

    recv2 = send(run_pack(blocks, summed0, 1, 0, bs, 0))

    slabs, corner, own1, sib1 = run_assemble(core, flags[0], recv1, swap(recv1[:, half - 8:]), half)
    sib1 = swap(sib1)
    head = jnp.linalg.cholesky(corner)
    solved = lax.linalg.triangular_solve(
        head, slabs.reshape(24 * bs, bs), left_side=False, lower=True, transpose_a=True
    )
    edge = jnp.stack([ji == 0, col == 0, t == 1]).astype(jnp.int32)
    out, rest, based = run_base(edge, front, solved, head, (own0, sib0, own1, sib1), bs)

    sib2, held2 = run_late_sums(flags[1], recv2, based)
    sib2 = swap(sib2)
    out, others = run_add_own(flags[1], out.reshape(2, 4, 2 * bs, cols_dev), rest, held2)
    return run_add_late(out, others, sib2).reshape(rows_dev, cols_dev)


def solution(mesh):
    fine = Mesh(mesh.devices.reshape(4, 2, 4, 2, 2), ALL)
    spec = P(("y", "zh"), ("x", "zl", "core"))
    return jax.shard_map(body, mesh=fine, in_specs=(spec, spec, P()), out_specs=spec, check_vma=False)
```

```python
import jax
import jax.numpy as jnp
from jax import lax
from jax.experimental import pallas as pl
from jax.experimental.pallas import tpu as pltpu
from jax.sharding import Mesh
from jax.sharding import PartitionSpec as P

CHIP = ("y", "zh", "x", "zl")
ALL = CHIP + ("core",)
CORE_SWAP = [(0, 1), (1, 0)]
VMEM = pl.BlockSpec(memory_space=pltpu.VMEM)
SMEM = pl.BlockSpec(memory_space=pltpu.SMEM)
HBM = pl.BlockSpec(memory_space=pltpu.HBM)
ANY = pl.BlockSpec(memory_space=pl.ANY)
F32 = jnp.float32


def call(kernel, out_shape, in_specs, out_specs, name, moved, scratch=(), aliases=None, limit=16):
    many = isinstance(out_shape, tuple)
    outs = zip(out_shape, out_specs) if many else ((out_shape, out_specs),)
    outs = tuple(pltpu.HBM(array.shape, array.dtype) if spec is HBM else array for array, spec in outs)
    run = pl.pallas_call(
        kernel,
        out_shape=outs if many else outs[0],
        in_specs=in_specs,
        out_specs=out_specs,
        scratch_shapes=scratch,
        input_output_aliases=aliases or {},
        compiler_params=pltpu.CompilerParams(vmem_limit_bytes=limit << 20),
        cost_estimate=pl.CostEstimate(flops=0, bytes_accessed=moved, transcendentals=0),
        name=name,
    )

    def placed(*args):
        return run(*(
            pltpu.with_memory_space_constraint(arg, pltpu.HBM) if spec is HBM else arg
            for arg, spec in zip(args, in_specs)
        ))

    return placed


def shape(*dims):
    return jax.ShapeDtypeStruct(dims, F32)


TOKEN = shape(8, 128)


def run_lift(updates, front, bs):
    rows = updates.shape[0]
    half = bs // 2

    cuts = 4
    some = half // cuts

    def lift(updates, front, low, high, token, ucol, fcol, sems):
        def read(i, cut, core):
            whole, part = ((updates, ucol), (front, fcol))[i]
            here = pl.ds(core * half + cut * some, some)
            return pltpu.make_async_copy(
                whole.at[:, here, pl.ds(0, bs)], part.reshape(17, bs, bs).at[pl.ds(0, 16), here], sems.at[i, cut, core]
            )

        pieces = [(i, cut, core) for cut in range(cuts) for i in range(2) for core in range(2)]
        for piece in pieces:
            read(*piece).start()
        token[...] = jnp.zeros_like(token)
        for i, cut, core in pieces:
            read(i, cut, core).wait()
            part, out = (ucol, fcol)[i], (low, high)[core]

            def one(n, carry):
                chip = cut * some + n
                out[chip, 16 * i:16 * i + 16] = part[pl.ds(core * half + chip, 16, stride=bs), :]
                return carry

            lax.fori_loop(0, some, one, 0, unroll=8)

    share = shape(half, 32, bs)
    blocks = (16, bs, updates.shape[1])
    return call(
        lift, (share, share, TOKEN), [HBM, HBM], (VMEM,) * 3, "lift", 16 * rows * bs,
        [pltpu.VMEM((rows + bs, bs), F32)] * 2 + [pltpu.SemaphoreType.DMA((2, cuts, 2))],
    )(updates.reshape(blocks), front.reshape(blocks))


def run_pack(blocks, wait, gi, at, rows, extra, child_map=None):
    bs = blocks.shape[1]
    more = child_map is not None

    def pack(blocks, wait, *rest):
        out = rest[1] if more else rest[0]
        held, parted, read_sems, write_sems = rest[-4:]

        def read(j):
            return pltpu.make_async_copy(blocks.at[8 * gi + j, pl.ds(at, rows)], held.at[j], read_sems.at[j])

        def write(j):
            some = pl.ds(8 * j, 8)
            return pltpu.make_async_copy(parted.at[some], out.at[some, pl.ds(0, rows)], write_sems.at[j])

        for j in range(8):
            read(j).start()
        if more:
            whole_map, _, ends, adds, entries, sems = rest[:6]
            last = pltpu.make_async_copy(blocks.at[pl.ds(0, 8), pl.ds(bs - 8, 8)], ends, sems.at[0])
            fetch = pltpu.make_async_copy(whole_map, entries, sems.at[1])
            last.start()
            fetch.start()
        for j in range(8):
            read(j).wait()
            for jc in range(8):
                parted[8 * j + jc] = held[j, :, jc * bs:(jc + 1) * bs]
            write(j).start()
        if more:
            y, zh, x, zl, _ = (lax.axis_index(a) for a in ALL)
            me, col_pair = 2 * y + zh, 2 * x + zl
            last.wait()
            fetch.wait()
            live = (col_pair == 0) & (entries[me // 4, 0] // 8 % 2 == 0)
            place = lax.broadcasted_iota(jnp.int32, (16, bs), 0)
            for g in range(2):
                group = 2 * (me % 4) + g
                to = jnp.where(live, 8 * (entries[me // 4, 8 * group + me] // 8 % 2) + group, -1)
                adds[g] = jnp.where(place == to, 1.0, 0.0)
        for j in range(8):
            write(j).wait()

    load = shape(64, rows + extra, bs)
    scratch = [
        pltpu.VMEM((8, rows, 8 * bs), F32), pltpu.VMEM((64, rows, bs), F32), pltpu.SemaphoreType.DMA((8,)),
        pltpu.SemaphoreType.DMA((8,)),
    ]
    if not more:
        return call(pack, load, [HBM, VMEM], HBM, "pack", 512 * rows * bs, scratch)(blocks, wait)
    return call(
        pack, (load, shape(8, 8, 8 * bs), shape(2, 16, bs)), [HBM, VMEM, HBM], (HBM, VMEM, VMEM), "pack", 512 * rows * bs,
        [pltpu.SMEM(child_map.shape, jnp.int32), pltpu.SemaphoreType.DMA((2,))] + scratch,
    )(blocks, wait, child_map)


def run_put_rows(adds, ends, load, low, other, rows):
    bs = low.shape[-1]

    def put_rows(adds, ends, load, low, other, out, token, region, sems):
        y, zh, x, zl, t = (lax.axis_index(a) for a in ALL)
        me, col_pair = 2 * y + zh, 2 * x + zl
        token[...] = jnp.zeros_like(token)
        slot = pl.ds(jnp.where(col_pair == 4, slot_of(0, 4), slot_of(me, 0)), 1)
        copies = []
        for j in range(8):
            some = slice(8 * j, 8 * j + 8)
            region[some] = jnp.where(t == 0, low[some], other[some])
            for jc in range(8):
                at = 8 * j + jc
                own = [region[at, pl.ds(8 * g + me, 1), :] for g in range(2)]
                region[at, 16:32] += adds[0] * own[0] + adds[1] * own[1]
                region[at, slot, :] = ends[j, 7:8, jc * bs:(jc + 1) * bs]
            some = pl.ds(8 * j, 8)
            copies.append(pltpu.make_async_copy(region.at[some], out.at[some, pl.ds(rows, 32)], sems.at[j]))
            copies[-1].start()
        for copy in copies:
            copy.wait()

    return call(
        put_rows, (shape(*load.shape), TOKEN), [VMEM, VMEM, HBM, VMEM, VMEM], (HBM, VMEM), "put_rows", 8 * other.size,
        [pltpu.VMEM(low.shape, F32), pltpu.SemaphoreType.DMA((8,))], aliases={2: 0},
    )(adds, ends, load, low, other)


def run_sum_rows(marks, recv, ends, load, first):
    bs = recv.shape[-1]
    last = load.shape[1] - 40

    def sum_rows(marks, recv, ends, load, out, token, kids, total, rows, sems):
        token[...] = jnp.zeros_like(token)
        for up in range(2):
            for sr in range(4):
                acc = jnp.zeros((16, bs), F32)
                for h in range(2):
                    for v in range(2):
                        acc += marks[up, sr, 2 * v + h] * recv[(4 * h + sr) * 8 + 4 * v, first:first + 16]
                kids[pl.ds((up * 4 + sr) * 16, 16)] = acc
        for j in range(8):
            total[j] = kids[pl.ds(j, 16, stride=8), :] + recv[8 * j, first + 16:first + 32]
        copies = []
        for j in range(8):
            for jc in range(8):
                at = 8 * j + jc
                rows[at, 0:8] = ends[j, :, jc * bs:(jc + 1) * bs]
                rows[at, 7:8] = total[0, 0:1]
                rows[at, 8:24] = total[j]
                rows[at, 24:40] = total[jc]
            some = pl.ds(8 * j, 8)
            copies.append(pltpu.make_async_copy(rows.at[some], out.at[some, pl.ds(last, 40)], sems.at[j]))
            copies[-1].start()
        for copy in copies:
            copy.wait()

    return call(
        sum_rows, (shape(*load.shape), TOKEN), [VMEM, VMEM, VMEM, HBM], (HBM, VMEM), "sum_rows", 64 * 40 * bs * 8,
        [
            pltpu.VMEM((136, bs), F32), pltpu.VMEM((8, 16, bs), F32), pltpu.VMEM((64, 40, bs), F32),
            pltpu.SemaphoreType.DMA((8,)),
        ],
        aliases={3: 0},
    )(marks, recv, ends, load)


def add_blocks(flags, recv, sr, scp, here, sides, behind=None):
    sums = {}
    for h in range(2):
        for v in range(2):
            source, col_pair = 4 * h + sr, 4 * v + scp
            rows = here if behind is None else pl.ds(behind + slot_of(source, col_pair), 1)
            block = recv[source * 8 + col_pair, rows]
            for up in range(2):
                for side in sides:
                    term = flags[((((h + 2 * v) * 4 + sr) * 4 + scp) * 2 + up) * 2 + side] * block
                    sums[up, side] = sums[up, side] + term if (up, side) in sums else term
    return sums


def slot_of(row, col_pair):
    return 16 if col_pair == 4 else 8 + row


def child_sums(flags, recv, outs, held, sems, rows):
    step = 32
    more = held[0].shape[3] > rows

    def write(side, sr):
        return pltpu.make_async_copy(held[side].at[:, sr], outs[side].at[:, sr], sems.at[side, sr])

    for sr in range(4):
        def one(i, carry):
            at = pl.multiple_of(i * step, step)
            for scp in range(4):
                sums = add_blocks(flags, recv, sr, scp, pl.ds(at, step), (0, 1))
                for up in range(2):
                    for side in range(2):
                        held[side][up, sr, scp, pl.ds(at, step)] = sums[up, side]
            return carry

        lax.fori_loop(0, rows // step, one, 0)
        for scp in range(4) if more else ():
            sums = add_blocks(flags, recv, sr, scp, None, (0, 1), rows)
            for up in range(2):
                for side in range(2):
                    held[side][up, sr, scp, rows:rows + 1] = sums[up, side]
        for side in range(2):
            write(side, sr).start()

    def finish():
        for sr in range(4):
            for side in range(2):
                write(side, sr).wait()

    return finish


def sums_scratch(rows, bs):
    return [pltpu.VMEM((2, 4, 4, rows, bs), F32)] * 2 + [pltpu.SemaphoreType.DMA((2, 4))]


def run_child_sums(flags, recv, wait, rows, bs):
    def kernel(flags, recv, wait, own, sib, token, *held):
        token[...] = jnp.zeros_like(token)
        child_sums(flags, recv, (own, sib), held[:2], held[2], rows)()

    part = shape(2, 4, 4, rows + 8, bs)
    return call(
        kernel, (part, part, TOKEN), [SMEM, VMEM, VMEM], (HBM, HBM, VMEM), "child_sums", 64 * rows * bs * 8,
        sums_scratch(rows + 8, bs),
    )(flags, recv, wait)


def run_assemble(core, flags, mine, other, first):
    chips, width, bs = mine.shape
    half = bs // 2

    wide = width - first + 8

    def assemble(core, flags, mine, other, slabs, corner, own, sib, here, there, out, sems, *held):
        t = core[0]
        copies = [
            pltpu.make_async_copy(
                mine.at[:, pl.ds(first - 8, wide)], here.reshape(chips + 1, wide, bs).at[pl.ds(0, chips)], sems.at[0]
            ),
            pltpu.make_async_copy(other, there.reshape(chips + 1, wide, bs).at[pl.ds(0, chips)], sems.at[1]),
        ]
        for copy in copies:
            copy.start()
        finish = child_sums(flags, mine, (own, sib), held[:2], held[2], first)
        for who, (copy, part) in enumerate(zip(copies, (here, there))):
            copy.wait()
            rows_at = pl.multiple_of(half * (t if who == 0 else 1 - t), half)
            for s in range(25):
                start = 8 + s if s < 16 else 8 + s + 8 * t if s < 24 else 7
                rows = part[pl.ds(start, half, stride=wide), :]
                if s < 24:
                    out[s, pl.ds(rows_at, half)] = rows
                else:
                    corner[pl.ds(rows_at, half)] = rows
        copy = pltpu.make_async_copy(out, slabs, sems.at[2])
        copy.start()
        finish()
        copy.wait()

    part = shape(2, 4, 4, first, bs)
    return call(
        assemble, (shape(24, bs, bs), shape(bs, bs), part, part), [SMEM, SMEM, VMEM, ANY], (HBM, VMEM, HBM, HBM),
        "assemble", 200 * bs * bs,
        [pltpu.VMEM(((chips + 1) * wide, bs), F32)] * 2 + [pltpu.VMEM((24, bs, bs), F32), pltpu.SemaphoreType.DMA((3,))]
        + sums_scratch(first, bs),
    )(core, flags, mine, other)


def split(a):
    high = a.astype(jnp.bfloat16)
    left = a - high.astype(F32)
    mid = left.astype(jnp.bfloat16)
    return high, mid, (left - mid.astype(F32)).astype(jnp.bfloat16)


def spread(left, mine, other):
    return jnp.where(left, mine, other), jnp.where(left, other, mine)


def pair(scp, bs):
    return slice(2 * scp * bs, (2 * scp + 1) * bs), slice((2 * scp + 1) * bs, (2 * scp + 2) * bs)


def run_base(edge, front, solved, head, early, bs):
    rows, cols = front.shape
    blocks, tile, step = rows // bs, 256, 32
    cut = early[0].shape[3] - 8

    group = 4

    def base(edge, front, solved, head, own0, sib0, own1, sib1, out, rest, token, held, right, o0, s0, o1, s1, sems, more, back, parts_back):
        top, col_zero, left = edge[0] == 1, edge[1] == 1, edge[2] == 0
        token[...] = jnp.zeros_like(token)

        def read(i):
            return pltpu.make_async_copy(front.at[i], held.at[i], sems.at[i])

        def write(n):
            return pltpu.make_async_copy(held.at[2 * n], out.at[n, pl.ds(0, bs)], back.at[n])

        def part(n, c):
            return pltpu.make_async_copy(held.at[2 * n + 1, :, pl.ds(c * bs, bs)], rest.at[c, n], parts_back.at[c, n])

        sums = [
            pltpu.make_async_copy(src, dst, more.at[n])
            for n, (src, dst) in enumerate(((own0, o0), (sib0, s0), (own1, o1), (sib1, s1)))
        ]
        for i in range(blocks):
            read(i).start()
            if i == group - 1:
                for copy in sums:
                    copy.start()

        for at in range(0, cols, bs):
            high, mid, low = split(solved[rows + at:rows + at + bs])
            right[at:at + bs] = jnp.concatenate([high, high, mid, high, mid, low], axis=1)

        def some(q, carry):
            own = solved[pl.ds(pl.multiple_of(q * group * bs, group * bs), group * bs)]
            high, mid, low = split(own)
            parts = jnp.concatenate([high, mid, high, low, mid, high], axis=1)
            for n in range(group):
                read(q * group + n).wait()
            for at in range(0, cols, tile):
                lanes = slice(at, at + tile)
                product = lax.dot_general(
                    parts, right[at:at + tile], (((1,), (1,)), ((), ())), preferred_element_type=F32
                )
                for n in range(group):
                    keep = jnp.where(top & (q == 0), 0.0, 1.0) if n == 0 else 1.0
                    held[q * group + n, :, lanes] -= keep * product[n * bs:(n + 1) * bs]

            @pl.when(col_zero)
            def _():
                for n in range(group):
                    held[q * group + n, :, 0:bs] = own[n * bs:(n + 1) * bs]

            @pl.when(top & col_zero & (q == 0))
            def _():
                held[0, :, 0:bs] = head[...]

            @pl.when(q == 0)
            def _():
                for copy in sums:
                    copy.wait()
                for late, soon in ((o1, o0), (s1, s0)):
                    late[:, :, :, bs - cut - 1:bs - cut] = soon[:, :, :, cut:cut + 1]

            for n in range(0, group, 2):
                i = q * group + n
                up, sr = i // 8, i // 2 % 4
                for at in range(0, bs, step):
                    here = slice(at, at + step)
                    own, sib, inner = (o0, s0, at) if at < cut else (o1, s1, at - cut)
                    for scp in range(4):
                        two = spread(left, own[up, sr, scp, inner:inner + step], sib[up, sr, scp, inner:inner + step])
                        for lanes, add in zip(pair(scp, bs), two):
                            held[i, here, lanes] += add
                write(i // 2).start()
                for c in range(cols // bs):
                    part(i // 2, c).start()
            return carry

        lax.fori_loop(0, blocks // group, some, 0)

        def finish(n, carry):
            write(n).wait()
            for c in range(cols // bs):
                part(n, c).wait()
            return carry

        lax.fori_loop(0, blocks // 2, finish, 0)

    parts = [pltpu.VMEM(a.shape, F32) for a in early]
    return call(
        base, (shape(blocks // 2, 2 * bs, cols), shape(cols // bs, blocks // 2, bs, bs), TOKEN), [SMEM, HBM, VMEM, VMEM] + [ANY] * 4,
        (HBM, HBM, VMEM), "base", rows * cols * 8,
        [pltpu.VMEM((blocks, bs, cols), F32), pltpu.VMEM((cols, 6 * bs), jnp.bfloat16)] + parts
        + [pltpu.SemaphoreType.DMA(n) for n in ((blocks,), (4,), (blocks // 2,), (cols // bs, blocks // 2))],
        limit=28,
    )(edge, front.reshape(blocks, bs, cols), solved, head, *early)


def run_late_sums(flags, recv, wait):
    chips, bs, _ = recv.shape
    step, cuts = 32, 2
    part = bs // cuts

    def late_sums(all_flags, recv, wait, sib, held, flags, flag_sem, sems):
        fetch = pltpu.make_async_copy(all_flags, flags, flag_sem)
        fetch.start()

        def read(sr, cut, h):
            some, here = pl.ds((4 * h + sr) * 8, 8), pl.ds(cut * part, part)
            return pltpu.make_async_copy(recv.at[some, here], held.at[some, here], sems.at[sr, cut, h])

        pieces = [(sr, cut) for sr in range(4) for cut in range(cuts)]
        for sr, cut in pieces:
            for h in range(2):
                read(sr, cut, h).start()
        fetch.wait()
        for sr, cut in pieces:
            for h in range(2):
                read(sr, cut, h).wait()

            def one(i, carry):
                here = pl.ds(pl.multiple_of(cut * part + i * step, step), step)
                for scp in range(4):
                    sums = add_blocks(flags, held, sr, scp, here, (1,))
                    for up in range(2):
                        sib[up, sr, scp, here] = sums[up, 1]
                return carry

            lax.fori_loop(0, part // step, one, 0)

    return call(
        late_sums, (shape(2, 4, 4, bs, bs), shape(*recv.shape)), [HBM, HBM, VMEM], (VMEM, VMEM), "late_sums", 96 * bs * bs * 4,
        [
            pltpu.SMEM(flags.shape, F32), pltpu.SemaphoreType.DMA,
            pltpu.SemaphoreType.DMA((4, cuts, 2)),
        ],
    )(flags, recv, wait)


def run_add_own(flags, out, rest, recv):
    bs, step = recv.shape[1], 32
    parts = rest.reshape(8, 2, 4, bs, bs)

    def add_own(all_flags, before, rest, held, out, others, flags, mine, flag_sem, own_sems, other_sems, back):
        fetch = pltpu.make_async_copy(all_flags, flags, flag_sem)
        fetch.start()
        t = lax.axis_index("core")

        def own(scp):
            return pltpu.make_async_copy(rest.at[2 * scp + t], mine.at[scp], own_sems.at[scp])

        def other(scp):
            return pltpu.make_async_copy(rest.at[2 * scp + 1 - t], others.at[scp], other_sems.at[scp])

        def write(sr, scp):
            lanes = pl.ds(pl.multiple_of((2 * scp + t) * bs, bs), bs)
            return pltpu.make_async_copy(mine.at[scp, :, sr], out.at[:, sr, pl.ds(bs, bs), lanes], back.at[sr, scp])

        for scp in range(4):
            own(scp).start()
        for scp in range(4):
            other(scp).start()
        fetch.wait()
        for scp in range(4):
            own(scp).wait()
        for sr in range(4):
            def one(i, carry):
                here = pl.ds(pl.multiple_of(i * step, step), step)
                for scp in range(4):
                    sums = add_blocks(flags, held, sr, scp, here, (0,))
                    for up in range(2):
                        mine[scp, up, sr, here] += sums[up, 0]
                return carry

            lax.fori_loop(0, bs // step, one, 0)
            for scp in range(4):
                write(sr, scp).start()
        for scp in range(4):
            other(scp).wait()
            for sr in range(4):
                write(sr, scp).wait()

    half = (4, 2, 4, bs, bs)
    return call(
        add_own, (shape(*out.shape), shape(*half)), [HBM] * 3 + [VMEM], (HBM, VMEM), "add_own", rest.size * 12,
        [pltpu.SMEM(flags.shape, F32), pltpu.VMEM(half, F32), pltpu.SemaphoreType.DMA]
        + [pltpu.SemaphoreType.DMA(n) for n in ((4,), (4,), (4, 4))],
        aliases={1: 0},
    )(flags, out, parts, recv)


def run_add_late(out, others, sib):
    bs, step = sib.shape[-1], 32

    def add_late(before, others, sib, out, done, sems):
        t = lax.axis_index("core")

        def write(scp, up):
            lanes = pl.ds(pl.multiple_of((2 * scp + 1 - t) * bs, bs), bs)
            return pltpu.make_async_copy(done.at[scp, up], out.at[up, :, pl.ds(bs, bs), lanes], sems.at[scp, up])

        for scp in range(4):
            for up in range(2):
                for sr in range(4):
                    for at in range(0, bs, step):
                        here = slice(at, at + step)
                        done[scp, up, sr, here] = others[scp, up, sr, here] + sib[up, sr, scp, here]
                write(scp, up).start()
        for scp in range(4):
            for up in range(2):
                write(scp, up).wait()

    return call(
        add_late, shape(*out.shape), [HBM, VMEM, VMEM], HBM, "add_late", others.size * 12,
        [pltpu.VMEM(others.shape, F32), pltpu.SemaphoreType.DMA((4, 2))], aliases={0: 0},
    )(out, others, sib)


def body(front, updates, child_map):
    rows_dev, cols_dev = front.shape
    bs = rows_dev // 16
    half = bs // 2
    y, zh, x, zl, t = (lax.axis_index(a) for a in ALL)
    ji, jc = 2 * y + zh, 2 * x + zl
    col = 2 * jc + t
    core = t.reshape(1).astype(jnp.int32)
    blocks = updates.reshape(16, bs, cols_dev)

    def swap(a):
        return lax.ppermute(a, "core", CORE_SWAP)

    def send(load):
        return lax.all_to_all(load, CHIP, 0, 0, tiled=True)

    bits = (child_map.reshape(4, 8, 8) // 8) % 2
    col_bits = lax.dynamic_index_in_dim(bits, jc, 2, keepdims=False).reshape(4, 4, 2)
    col_bits = lax.dynamic_index_in_dim(col_bits, t, 2, keepdims=False)
    row_bits = lax.dynamic_index_in_dim(bits, ji, 2, keepdims=False).reshape(4, 4, 2)
    in_panel = (col == 0) & (jnp.arange(4) == 0)
    side = jnp.stack([(col_bits == t) & ~in_panel, col_bits != t], -1)
    up = row_bits[..., None] == jnp.arange(2)
    flags = [
        (up[:, :, gi, None, :, None] & side[:, None, :, None, :]).astype(F32).reshape(-1) for gi in range(2)
    ]
    live = bits[:, 0, 0] == 0
    marks = (bits.reshape(4, 4, 16).transpose(1, 0, 2) == jnp.arange(2)[:, None, None, None]) & live[:, None]
    sr_at, h_at, j_at = jnp.arange(4)[:, None, None], jnp.arange(4)[None, :, None], jnp.arange(16)[None, None] % 8
    marks &= ~((h_at < 2) & (4 * h_at + sr_at == j_at))
    marks = jnp.broadcast_to(marks.astype(F32)[..., None], (2, 4, 4, 16, bs))

    low, high, lifted = run_lift(updates, front, bs)
    other = lax.ppermute(high, ALL, [((r * 8 + q) * 2, (r * 8 + q) * 2 + 1) for r in range(8) for q in (0, 4)])
    load0, ends, adds = run_pack(blocks, lifted, 0, 0, half, 32, child_map)
    load0, sent0 = run_put_rows(adds, ends, load0, low, other, half)
    recv0 = send(load0)

    load1, sent1 = run_sum_rows(marks, recv0, ends, run_pack(blocks, sent0, 0, half, half, 32), half)
    recv1 = send(load1)
    own0, sib0, summed0 = run_child_sums(flags[0], recv0, sent1, half, bs)
    sib0 = swap(sib0)

    recv2 = send(run_pack(blocks, summed0, 1, 0, bs, 0))

    slabs, corner, own1, sib1 = run_assemble(core, flags[0], recv1, swap(recv1[:, half - 8:]), half)
    sib1 = swap(sib1)
    head = jnp.linalg.cholesky(corner)
    solved = lax.linalg.triangular_solve(
        head, slabs.reshape(24 * bs, bs), left_side=False, lower=True, transpose_a=True
    )
    edge = jnp.stack([ji == 0, col == 0, t == 1]).astype(jnp.int32)
    out, rest, based = run_base(edge, front, solved, head, (own0, sib0, own1, sib1), bs)

    sib2, held2 = run_late_sums(flags[1], recv2, based)
    sib2 = swap(sib2)
    out, others = run_add_own(flags[1], out.reshape(2, 4, 2 * bs, cols_dev), rest, held2)
    return run_add_late(out, others, sib2).reshape(rows_dev, cols_dev)


def solution(mesh):
    fine = Mesh(mesh.devices.reshape(4, 2, 4, 2, 2), ALL)
    spec = P(("y", "zh"), ("x", "zl", "core"))
    return jax.shard_map(body, mesh=fine, in_specs=(spec, spec, P()), out_specs=spec, check_vma=False)
```
